512 devices in a mesh: dp: 32 (over y, x), vocab: 16 (over z, core).
Axes of the slice: x: 4, y: 8, z: 8, core: 2. Of those that a mesh axis runs over, the one named last changes fastest.
Arguments:
- hidden: bfloat16 [256, 4608], P('dp'), may hold values from -6 to 6
- labels: int32 [256], replicated, may hold values from 0 to 255999
- head_weight: bfloat16 [256000, 4608], P(('dp', 'vocab')), may hold values from -1 to 1
- factor_rows: float32 [4608, 4608], P(('dp', 'vocab')), may hold values from -0.0002 to 16, as said below
Outputs:
- new_factor: float32 [4608, 4608], P(('dp', 'vocab'))
- gradients: bfloat16 [256, 4608], P('dp', 'vocab')
The draws below stay inside these ranges and needn't reach their ends.
Inputs may be any that keep to these rules, and one draw needn't show every extreme that they name: factor_rows is symmetric and positive definite.
All inputs are finite; a program needn't handle non-finite values.
Results may differ from the reference program's by a relative error of at most 0.0037.
Values may be sent and summed in bfloat16 or wider, within the bound.
A program may use at most 64 MiB of HBM per device.

```python
import math
import jax
import jax.numpy as jnp
from jax import lax

D = 4608
VOCAB = 256000
TOKENS = 256


def draw_factor_rows(key, part):
    key = jax.random.fold_in(key, 7)
    key_off, key_diag = jax.random.split(key)
    spread = jax.random.uniform(key_off, (D, D), jnp.float32, -1.0, 1.0)
    diagonal = jnp.exp(jax.random.uniform(key_diag, (D,), jnp.float32, 0.0, math.log(10.0)))
    off_part = 0.0002 * 0.5 * (spread + spread.T)
    row_ids = lax.broadcasted_iota(jnp.int32, (D, D), 0)
    col_ids = lax.broadcasted_iota(jnp.int32, (D, D), 1)
    return jnp.where(row_ids == col_ids, diagonal[:, None], off_part)


def set_ends(result, stream_key, smallest, top_value):
    spot = [jax.random.randint(jax.random.fold_in(stream_key, axis), (), 0, length) for axis, length in enumerate(result.shape)]
    widest = result.shape.index(max(result.shape))
    beside = spot[:widest] + [(spot[widest] + 1) % result.shape[widest]] + spot[widest + 1:]
    return result.at[tuple(spot)].set(smallest).at[tuple(beside)].set(top_value)


def with_spikes(values, own_key, source, target, shards_of, factor):
    owner, partner = [(jnp.arange(values.shape[position]) // (values.shape[position] // shards_of)).reshape([-1 if axis == position else 1 for axis in range(values.ndim)]) for position in (source, target)]
    chosen = jax.random.permutation(own_key, shards_of)[partner]
    strong = (owner == chosen) | (owner == (partner + shards_of // 2) % shards_of)
    return jnp.where(strong, factor * values, values)


def steps_of(key, dims, cuts, least, top_value):
    factor_of, own = 1.0, jax.random.fold_in(key, 6)
    for axis_at, blocks in cuts:
        steps = jnp.exp(jax.random.uniform(jax.random.fold_in(own, axis_at), (blocks,), jnp.float32, least / len(cuts), top_value / len(cuts)))
        factor_of = factor_of * jnp.repeat(steps, dims[axis_at] // blocks).reshape([-1 if axis == axis_at else 1 for axis in range(len(dims))])
    return factor_of


def normal_values(rng, shape, scale, reach, cuts=(), kind=jnp.bfloat16):
    factor_of = steps_of(rng, shape, cuts, -0.22, 0.18) if cuts else 1.0
    values = jax.random.normal(rng, shape, jnp.float32) * scale * factor_of
    return jnp.minimum(jnp.maximum(values, -reach), reach).astype(kind)


def heavy_noise(own_key, shape, width, bound, cuts, heavy, kind=jnp.bfloat16):
    result = width * jax.random.normal(own_key, shape, jnp.float32)
    if cuts:
        result = result * steps_of(own_key, shape, cuts, -0.22, 0.18)
    return jnp.clip(with_spikes(result, jax.random.fold_in(own_key, 3), *heavy), -bound, bound).astype(kind)


def setup_inputs(seed: int = 0) -> dict:
    streams_of = jax.random.split(jax.random.key(seed), 5)
    hidden = normal_values(streams_of[0], (TOKENS, D), 1.0, 6.0, ((0, 32),))
    labels = set_ends(jax.random.randint(streams_of[1], (TOKENS,), 0, VOCAB), jax.random.fold_in(streams_of[1], 1), 0, VOCAB - 1).astype(jnp.int32)
    head_weight = heavy_noise(streams_of[2], (VOCAB, D), (D // 9) ** -0.5, 1.0, ((0, 512),), (0, 1, 512, 6.0))
    factor_rows = draw_factor_rows(jax.random.fold_in(streams_of[4], 71), 0)
    return {"hidden": hidden, "labels": labels, "head_weight": head_weight, "factor_rows": factor_rows}


softcap = 30.0
decay_rate = 0.95


def reference(hidden, labels, head_weight, factor_rows):
    raw_logits = jnp.dot(hidden, head_weight.T, preferred_element_type=jnp.float32)
    squash = jnp.tanh(raw_logits / softcap)
    exp_terms = jnp.exp(softcap * squash)
    denominator = jnp.sum(exp_terms, axis=1, keepdims=True)
    columns = jnp.arange(VOCAB, dtype=jnp.int32)
    onehot = (columns[None, :] == labels.astype(jnp.int32)[:, None]).astype(jnp.float32)
    logit_grad = ((exp_terms / denominator - onehot) * (1.0 - squash * squash)).astype(jnp.bfloat16)
    gradients = jnp.dot(logit_grad, head_weight, preferred_element_type=jnp.float32).astype(jnp.bfloat16)
    gram_rows = lax.dot_general(gradients, gradients, (((0,), (0,)), ((), ())), preferred_element_type=jnp.float32)
    new_factor = decay_rate * factor_rows + (1.0 - decay_rate) * (D / TOKENS) * gram_rows
    return (new_factor, gradients)
```

```python
import jax
import jax.numpy as jnp
from jax import lax
from jax.experimental import pallas as pl
from jax.experimental.pallas import tpu as pltpu
from jax.sharding import PartitionSpec as P

softcap = 30.0
decay_rate = 0.95

NX, NY, NZ, NC = 4, 8, 8, 2
PLANE, LINE = NX * NY, NZ * NC
D, TOKENS, ROWS = 4608, 256, 500
PADDED = 512
HALF = D // 2
CHUNK = D // LINE
UNITS = CHUNK // 8 // NX
XU = 6
MESH = pl.DeviceIdType.MESH
f32, bf16 = jnp.float32, jnp.bfloat16


def kernel(
    hidden, labels, head, factor, new_factor, grads,
    wv, wt, hb, h2, lt, ds_, dr_, px, pz, rx, rz, qx, qz, r2x, r2z, ry, gb, rb, tb, rt, den_a, den_b,
    w_sem, hs, hr, hds, hdr, das, dar, dbs, dbr, c_s, c_r, xs, xr, zs, zr, x2s, x2r, z2s, z2r,
    ys, yr, gs, gr, bs, br, ts, tr,
):
    dp, vo = lax.axis_index("dp"), lax.axis_index("vocab")
    x, y = lax.rem(dp, NX), dp // NX
    c, z = lax.rem(vo, NC), vo // NC
    sib = vo + 1 - 2 * c

    def copy(src, dst, send, recv, to_dp, to_vo):
        return pltpu.make_async_remote_copy(
            src_ref=src, dst_ref=dst, send_sem=send, recv_sem=recv, device_id=(to_dp, to_vo), device_id_type=MESH
        )

    def got(ref, recv):
        copy(ref, ref, recv, recv, dp, sib).wait_recv()

    def sent(ref, send):
        copy(ref, ref, send, send, dp, sib).wait_send()

    def each(count, body):
        lax.fori_loop(1, count, lambda k, carry: (body(k), carry)[1], 0)

    def xp(k):
        return lax.rem(x + k, NX)

    def yp(k):
        return lax.rem(y + k + NY, NY)

    def zp(k):
        return lax.rem(z + k, NZ)

    def at_x(k):
        return y * NX + xp(k)

    def at_y(k):
        return yp(k) * NX + x

    def at_z(k):
        return zp(k) * NC + c

    w_copy = pltpu.make_async_copy(head, wv, w_sem)
    w_copy.start()
    gb[...] = jnp.zeros_like(gb)
    wt[:, PADDED - 128:] = jnp.zeros((D, 128), bf16)
    lt[PADDED - 16:, :] = jnp.zeros((16, TOKENS), bf16)

    barrier = pltpu.get_barrier_semaphore()
    each(LINE, lambda k: pl.semaphore_signal(
        barrier, inc=1, device_id=(dp, lax.rem(vo + k, LINE)), device_id_type=MESH))
    each(PLANE, lambda k: pl.semaphore_signal(
        barrier, inc=1, device_id=(lax.rem(dp + k, PLANE), vo), device_id_type=MESH))
    pl.semaphore_wait(barrier, LINE + PLANE - 2)

    def transpose_head(first, last):
        def body(b, carry):
            at = pl.multiple_of(b * 256, 256)
            wt[pl.ds(at, 256), 0:ROWS] = wv[:, pl.ds(at, 256)].T
            return carry

        lax.fori_loop(first, last, body, 0)

    @pl.when(c == 0)
    def _():
        hb[0, dp] = hidden[:, 0:HALF]
        for k in (1, 2, 3):
            copy(hb.at[0, dp], hb.at[0, dp], hs.at[k], hr.at[dp], at_x(k), vo).start()
        w_copy.wait()
        transpose_head(0, 6)
        for k in (1, 2, 3):
            got(hb.at[0, at_x(k)], hr.at[at_x(k)])

        def row(k):
            return hb.at[0, pl.ds(yp(k) * NX, NX)]

        def row_copy(from_k, to_k, sem):
            return copy(row(from_k), row(from_k), hs.at[sem], hr.at[yp(from_k) * NX], at_y(to_k), vo)

        def across(k):
            copy(row(k), row(k), hds.at[yp(k)], hdr.at[yp(k)], dp, sib).start()

        def row_got(k):
            got(row(k), hr.at[yp(k) * NX])

        row_copy(0, 1, 4).start()
        row_copy(0, -1, 5).start()
        row_copy(0, 4, 6).start()
        across(0)
        transpose_head(6, 12)
        row_got(-1)
        row_copy(-1, 1, 7).start()
        row_got(1)
        row_copy(1, -1, 8).start()
        across(-1)
        across(1)
        transpose_head(12, 18)
        row_got(4)
        row_copy(4, 1, 9).start()
        row_copy(4, -1, 10).start()
        across(4)
        for k in (2, -2, 3, -3):
            row_got(k)
            across(k)
        for k in (1, 2, 3):
            sent(hb.at[0, dp], hs.at[k])
        for sem in range(4, 11):
            sent(row(0), hs.at[sem])

    @pl.when(c == 1)
    def _():
        hb[1, dp] = hidden[:, HALF:]

        def own(k):
            return hb.at[1, at_y(k)]

        def spread(k):
            for i in (1, 2, 3):
                copy(own(k), own(k), hs.at[7 + yp(k) * 3 + i], hr.at[at_y(k)], yp(0) * NX + xp(i), vo).start()

        for k in (1, -1, 2, -2, 3, -3, 4):
            copy(own(0), own(0), hs.at[yp(k)], hr.at[dp], at_y(k), vo).start()
        spread(0)
        w_copy.wait()
        transpose_head(0, 12)
        for k in (1, -1, 2, -2, 3, -3, 4):
            got(own(k), hr.at[at_y(k)])
            spread(k)
        transpose_head(12, 18)

        def across(v, carry):
            for i in (1, 2, 3):
                slot = v * NX + xp(i)
                got(hb.at[1, slot], hr.at[slot])
            rows = hb.at[1, pl.ds(v * NX, NX)]
            copy(rows, rows, hds.at[v], hdr.at[v], dp, sib).start()
            return carry

        lax.fori_loop(0, NY, across, 0)
        for k in (1, -1, 2, -2, 3, -3, 4):
            sent(own(0), hs.at[yp(k)])
        for k in range(8, 32):
            sent(own(0), hs.at[k])

    def across_done(v, carry):
        got(hb.at[1 - c, pl.ds(v * NX, NX)], hdr.at[v])
        sent(hb.at[c, pl.ds(v * NX, NX)], hds.at[v])
        return carry

    lax.fori_loop(0, NY, across_done, 0)

    raw = jnp.zeros((ROWS, TOKENS), f32)
    for h in range(2):
        for part in range(2):
            width = HALF // 2
            h2[...] = hb[h, :, :, part * width:(part + 1) * width].astype(f32).reshape(TOKENS, width).astype(bf16)
            at = h * HALF + part * width
            raw += lax.dot_general(
                wv[:, at:at + width], h2[...], (((1,), (1,)), ((), ())), preferred_element_type=f32)
    squash = jnp.tanh(raw * (1.0 / softcap))
    terms = jnp.exp(softcap * squash)

    den_a[vo] = jnp.sum(terms, axis=0, keepdims=True)
    each(LINE, lambda k: copy(
        den_a.at[vo], den_a.at[vo], das.at[k], dar.at[vo], dp, lax.rem(vo + k, LINE)).start())
    each(LINE, lambda k: got(den_a.at[vo], dar.at[lax.rem(vo + k, LINE)]))
    each(LINE, lambda k: sent(den_a.at[vo], das.at[k]))
    den_b[dp] = jnp.sum(den_a[...], axis=0)
    each(PLANE, lambda k: copy(
        den_b.at[dp], den_b.at[dp], dbs.at[k], dbr.at[dp], lax.rem(dp + k, PLANE), vo).start())
    each(PLANE, lambda k: got(den_b.at[dp], dbr.at[lax.rem(dp + k, PLANE)]))
    each(PLANE, lambda k: sent(den_b.at[dp], dbs.at[k]))
    denominator = jnp.sum(den_b[...], axis=0)

    onehot = lax.broadcasted_iota(jnp.int32, (ROWS, TOKENS), 0) == labels[...] - (dp * LINE + vo) * ROWS
    lt[0:ROWS, :] = (
        (terms * (1.0 / denominator) - onehot.astype(f32)) * (1.0 - squash * squash)).astype(bf16)

    def partial_of(i, core):
        start = pl.multiple_of((i * NC + core) * CHUNK, 32)
        product = jnp.dot(wt[pl.ds(start, CHUNK), :], lt[...], preferred_element_type=f32)
        return product.reshape(NX, UNITS, 8, TOKENS)

    def first(i, carry):
        ds_[i] = partial_of(i, 1 - c).astype(bf16)
        copy(ds_.at[i], dr_.at[i], c_s.at[i], c_r.at[i], dp, sib).start()
        return carry

    lax.fori_loop(0, NZ, first, 0)
    for g in range(2):
        def second(i, carry, g=g):
            total = partial_of(i, c)
            got(dr_.at[i], c_r.at[i])
            total = (total + dr_[i].astype(f32)).astype(bf16)
            for v in range(NX):
                px[g, v, i - 4 * g] = total[v, 0:XU]
                pz[i, v] = total[v, XU:]

            @pl.when(i != z)
            def _():
                copy(pz.at[i], rz.at[z], zs.at[i], zr.at[z], dp, i * NC + c).start()

            return carry

        lax.fori_loop(4 * g, 4 * g + 4, second, 0)
        for k in (1, 2, 3):
            copy(px.at[g, xp(k)], rx.at[g, x], xs.at[g, k], xr.at[g, x], at_x(k), vo).start()

    each(NZ, lambda k: got(rz.at[0], zr.at[zp(k)]))
    total = pz[z].astype(f32)
    for k in range(1, NZ):
        total += rz[zp(k)].astype(f32)
    qz[...] = total.astype(bf16)
    for k in (1, 2, 3):
        copy(qz.at[xp(k)], r2z.at[x], z2s.at[k], z2r.at[x], at_x(k), vo).start()
    for g in range(2):
        total = px[g, x].astype(f32)
        for k in (1, 2, 3):
            got(rx.at[g, 0], xr.at[g, xp(k)])
            total += rx[g, xp(k)].astype(f32)
        qx[4 * g:4 * g + 4] = total.astype(bf16)
    each(NZ, lambda k: copy(
        qx.at[zp(k)], r2x.at[z], x2s.at[k], x2r.at[z], dp, at_z(k)).start())
    total = qz[x].astype(f32)
    for k in (1, 2, 3):
        got(r2z.at[0], z2r.at[xp(k)])
        total += r2z[xp(k)].astype(f32)
    ry[y, XU:] = total.astype(bf16)
    each(NZ, lambda k: got(r2x.at[0], x2r.at[zp(k)]))
    total = qx[z].astype(f32)
    for k in range(1, NZ):
        total += r2x[zp(k)].astype(f32)
    ry[y, 0:XU] = total.astype(bf16)

    each(NY, lambda k: copy(ry.at[y], ry.at[y], ys.at[k], yr.at[y], at_y(k), vo).start())
    each(NY, lambda k: got(ry.at[0], yr.at[yp(k)]))
    each(NY, lambda k: sent(ry.at[0], ys.at[k]))
    total = ry[0].astype(f32)
    for k in range(1, NY):
        total += ry[k].astype(f32)
    shift = lax.rem(vo, 4) * 4

    def quarter(v):
        return gb.at[pl.ds(shift + v * UNITS, UNITS)]

    gb[pl.ds(shift + x * UNITS, UNITS)] = total.astype(bf16)
    for k in (1, 2, 3):
        copy(quarter(x), quarter(x), gs.at[k], gr.at[x], at_x(k), vo).start()
    for k in (1, 2, 3):
        got(quarter(xp(k)), gr.at[xp(k)])
    for k in (1, 2, 3):
        sent(quarter(x), gs.at[k])

    source = y * NC + x // 2
    own_rows = gb.at[pl.ds(shift + lax.rem(x, 2) * 18, 18)]

    @pl.when(vo == source)
    def _():
        each(LINE, lambda k: copy(own_rows, rb, bs.at[k], br, dp, lax.rem(vo + k, LINE)).start())
        rb[...] = gb[pl.ds(shift + lax.rem(x, 2) * 18, 18)]
        each(LINE, lambda k: sent(rb, bs.at[k]))

    @pl.when(vo != source)
    def _():
        got(rb, br)

    rows = rb[...].astype(f32).reshape(144, TOKENS).astype(bf16)
    line_row = lax.broadcasted_iota(jnp.int32, (256, 144), 0)
    column = lax.broadcasted_iota(jnp.int32, (256, 144), 1)
    place, within = line_row // 16, lax.rem(line_row, 16)
    pick = jnp.where((within < 9) & (column == place * 9 + within), 1.0, 0.0).astype(bf16)
    spread_rows = jnp.dot(pick, rows, preferred_element_type=f32).astype(bf16)
    columns = gb[...].astype(f32).reshape(384, TOKENS).astype(bf16)
    gram = lax.dot_general(spread_rows, columns, (((1,), (1,)), ((), ())), preferred_element_type=f32)
    tb[...] = gram.reshape(LINE, 16, 384).astype(bf16)
    each(LINE, lambda k: copy(
        tb.at[lax.rem(vo + k, LINE)], rt.at[vo], ts.at[k], tr.at[vo], dp, lax.rem(vo + k, LINE)).start())

    block = gb[pl.ds(shift, 36)].astype(f32).reshape(CHUNK, TOKENS).astype(bf16)
    token = lax.broadcasted_iota(jnp.int32, (8, TOKENS), 1)
    mine = jnp.where(token == dp * 8 + lax.broadcasted_iota(jnp.int32, (8, TOKENS), 0), 1.0, 0.0).astype(bf16)
    grads[...] = lax.dot_general(
        mine, block, (((1,), (1,)), ((), ())), preferred_element_type=f32).astype(bf16)

    new_factor[...] = decay_rate * factor[...]
    rt[vo] = tb[vo]
    each(LINE, lambda k: got(rt.at[0], tr.at[lax.rem(vo + k, LINE)]))
    scale = (1.0 - decay_rate) * (D / TOKENS)
    for v in range(LINE):
        at = v * CHUNK // 128 * 128
        new_factor[:, at:at + 384] += scale * rt[v].astype(f32)[0:9]

    each(NZ, lambda k: sent(pz.at[0], zs.at[zp(k)]))
    each(NZ, lambda k: sent(qx.at[0], x2s.at[k]))
    for k in (1, 2, 3):
        sent(qz.at[0], z2s.at[k])
        for g in range(2):
            sent(px.at[g, 0], xs.at[g, k])
    lax.fori_loop(0, NZ, lambda i, carry: (sent(ds_.at[i], c_s.at[i]), carry)[1], 0)
    each(LINE, lambda k: sent(tb.at[0], ts.at[k]))


def on_device(hidden, labels, head_weight, factor_rows):
    vmem = pl.BlockSpec(memory_space=pltpu.VMEM)
    dma = pltpu.SemaphoreType.DMA

    def buf(*shape, dtype=bf16):
        return pltpu.VMEM(shape, dtype)

    return pl.pallas_call(
        kernel,
        out_shape=(
            jax.ShapeDtypeStruct(factor_rows.shape, f32),
            jax.ShapeDtypeStruct((TOKENS // PLANE, CHUNK), bf16),
        ),
        in_specs=[vmem, vmem, pl.BlockSpec(memory_space=pl.ANY), vmem],
        out_specs=(vmem, vmem),
        scratch_shapes=[
            buf(ROWS, D), buf(D, PADDED), buf(2, PLANE, 8, HALF), buf(TOKENS, HALF // 2), buf(PADDED, TOKENS),
            buf(NZ, NX, UNITS, 8, TOKENS), buf(NZ, NX, UNITS, 8, TOKENS),
            buf(2, NX, 4, XU, 8, TOKENS), buf(NZ, NX, UNITS - XU, 8, TOKENS),
            buf(2, NX, 4, XU, 8, TOKENS), buf(NZ, NX, UNITS - XU, 8, TOKENS),
            buf(NZ, XU, 8, TOKENS), buf(NX, UNITS - XU, 8, TOKENS),
            buf(NZ, XU, 8, TOKENS), buf(NX, UNITS - XU, 8, TOKENS),
            buf(NY, UNITS, 8, TOKENS), buf(48, 8, TOKENS), buf(18, 8, TOKENS),
            buf(LINE, 16, 384), buf(LINE, 16, 384),
            buf(LINE, 1, TOKENS, dtype=f32), buf(PLANE, 1, TOKENS, dtype=f32),
            dma, dma((32,)), dma((32,)), dma((8,)), dma((8,)),
            dma((LINE,)), dma((LINE,)), dma((PLANE,)), dma((PLANE,)), dma((NZ,)), dma((NZ,)),
            dma((2, NX)), dma((2, NX)), dma((NZ,)), dma((NZ,)), dma((NZ,)), dma((NZ,)), dma((NX,)), dma((NX,)),
            dma((NY,)), dma((NY,)), dma((NX,)), dma((NX,)), dma((LINE,)), dma, dma((LINE,)), dma((LINE,)),
        ],
        compiler_params=pltpu.CompilerParams(
            collective_id=0, has_side_effects=True, vmem_limit_bytes=56 * 2**20),
        cost_estimate=pl.CostEstimate(flops=4 * 500 * 256 * 4608, bytes_accessed=6 * 2**20, transcendentals=2 * 500 * 256),
    )(hidden, labels.reshape(1, TOKENS), head_weight, factor_rows)


def solution(mesh):
    placed = (P("dp", None), P(), P(("dp", "vocab"), None), P(("dp", "vocab"), None))
    return jax.shard_map(
        on_device,
        mesh=mesh,
        in_specs=placed,
        out_specs=(P(("dp", "vocab"), None), P("dp", "vocab")),
        check_vma=False,
    )
```

```python
import jax
import jax.numpy as jnp
from jax import lax
from jax.experimental import pallas as pl
from jax.experimental.pallas import tpu as pltpu
from jax.sharding import PartitionSpec as P

softcap = 30.0
decay_rate = 0.95

NX, NY, NZ, NC = 4, 8, 8, 2
PLANE, LINE = NX * NY, NZ * NC
D, TOKENS, ROWS = 4608, 256, 500
PADDED = 512
SHARE = D // 3
CHUNK = D // LINE
UNITS = CHUNK // 8 // NX
XU = 6
MESH = pl.DeviceIdType.MESH
f32, bf16 = jnp.float32, jnp.bfloat16


def kernel(
    hidden, labels, head, factor, new_factor, grads,
    wv, wt, hb0, hb1, h2, lt, ds_, dr_, px, pz, rx, rz, qx, qz, r2x, r2z, ry, gb, rb, tb, rt, den_a, den_b, lab, bds, bdr, bpx, bpz, brx, brz,
    w_sem, hs, hr, hds, hdr, das, dar, dbs, dbr, c_s, c_r, xs, xr, zs, zr, x2s, x2r, z2s, z2r,
    ys, yr, gs, gr, bs, br, ts, tr, gds, gdr, bc_s, bc_r, bxs, bxr, bzs, bzr,
):
    dp, vo = lax.axis_index("dp"), lax.axis_index("vocab")
    x, y = lax.rem(dp, NX), dp // NX
    c, z = lax.rem(vo, NC), vo // NC
    sib = vo + 1 - 2 * c

    def copy(src, dst, send, recv, to_dp, to_vo):
        return pltpu.make_async_remote_copy(
            src_ref=src, dst_ref=dst, send_sem=send, recv_sem=recv, device_id=(to_dp, to_vo), device_id_type=MESH
        )

    def got(ref, recv):
        copy(ref, ref, recv, recv, dp, sib).wait_recv()

    def sent(ref, send):
        copy(ref, ref, send, send, dp, sib).wait_send()

    def each(count, body):
        lax.fori_loop(1, count, lambda k, carry: (body(k), carry)[1], 0)

    def xp(k):
        return lax.rem(x + k, NX)

    def yp(k):
        return lax.rem(y + k + NY, NY)

    def zp(k):
        return lax.rem(z + k, NZ)

    def at_x(k):
        return y * NX + xp(k)

    def at_y(k):
        return yp(k) * NX + x

    def at_z(k):
        return zp(k) * NC + c

    w_copy = pltpu.make_async_copy(head, wv, w_sem)
    w_copy.start()
    gb[...] = jnp.zeros_like(gb)
    wt[:, PADDED - 128:] = jnp.zeros((D, 128), bf16)
    lt[PADDED - 16:, :] = jnp.zeros((16, TOKENS), bf16)
    lab[PADDED - 16:, :] = jnp.zeros((16, TOKENS), bf16)

    barrier = pltpu.get_barrier_semaphore()
    each(LINE, lambda k: pl.semaphore_signal(
        barrier, inc=1, device_id=(dp, lax.rem(vo + k, LINE)), device_id_type=MESH))
    each(PLANE, lambda k: pl.semaphore_signal(
        barrier, inc=1, device_id=(lax.rem(dp + k, PLANE), vo), device_id_type=MESH))
    holder_dp, holder_vo = y * NX + 2 * lax.rem(x, 2) + c, y * NC + x // 2
    taker_dp, taker_core = y * NX + 2 * c + x // 2, lax.rem(x, 2)
    holds = z == y
    own_taker = (taker_dp == dp) & (taker_core == c)

    @pl.when((holder_dp != dp) | (holder_vo != vo))
    def _():
        pl.semaphore_signal(barrier, inc=1, device_id=(holder_dp, holder_vo), device_id_type=MESH)

    takers = jnp.where(holds, NZ - jnp.where(own_taker, 1, 0), 0)
    pl.semaphore_wait(barrier, LINE + PLANE - 2 + takers)

    def transpose_head(first, last):
        def body(b, carry):
            at = pl.multiple_of(b * 256, 256)
            wt[pl.ds(at, 256), 0:ROWS] = wv[:, pl.ds(at, 256)].T
            return carry

        lax.fori_loop(first, last, body, 0)

    def partial_of(rows, i, core):
        start = pl.multiple_of((i * NC + core) * CHUNK, 32)
        product = jnp.dot(wt[pl.ds(start, CHUNK), :], rows[...], preferred_element_type=f32)
        return product.reshape(NX, UNITS, 8, TOKENS)

    def for_sibling(rows, out, arriving, s_sem, r_sem):
        def body(i, carry):
            out[i] = partial_of(rows, i, 1 - c).astype(bf16)
            copy(out.at[i], arriving.at[i], s_sem.at[i], r_sem.at[i], dp, sib).start()
            return carry

        lax.fori_loop(0, NZ, body, 0)

    def own_half(g, rows, arriving, r_sem, by_x, by_z, z_arriving, zs_sem, zr_sem):
        def body(i, carry):
            total = partial_of(rows, i, c)
            got(arriving.at[i], r_sem.at[i])
            total = (total + arriving[i].astype(f32)).astype(bf16)
            for v in range(NX):
                by_x[g, v, i - 4 * g] = total[v, 0:XU]
                by_z[i, v] = total[v, XU:]

            @pl.when(i != z)
            def _():
                copy(by_z.at[i], z_arriving.at[z], zs_sem.at[i], zr_sem.at[z], dp, i * NC + c).start()

            return carry

        lax.fori_loop(4 * g, 4 * g + 4, body, 0)

    def send_x(g, by_x, arriving, s_sem, r_sem):
        for k in (1, 2, 3):
            copy(by_x.at[g, xp(k)], arriving.at[g, x], s_sem.at[g, k], r_sem.at[g, x], at_x(k), vo).start()

    onehot = lax.broadcasted_iota(jnp.int32, (ROWS, TOKENS), 0) == labels[...] - (dp * LINE + vo) * ROWS

    def label_first():
        lab[0:ROWS, :] = onehot.astype(f32).astype(bf16)
        for_sibling(lab, bds, bdr, bc_s, bc_r)

    def label_second():
        for g in range(2):
            own_half(g, lab, bdr, bc_r, bpx, bpz, brz, bzs, bzr)

    @pl.when(c == 0)
    def _():
        hb0[dp] = hidden[:, 0:SHARE]
        for k in (1, 2, 3):
            copy(hb0.at[dp], hb0.at[dp], hs.at[k], hr.at[dp], at_x(k), vo).start()
        w_copy.wait()
        transpose_head(0, 18)
        for k in (1, 2, 3):
            got(hb0.at[at_x(k)], hr.at[at_x(k)])

        def row(k):
            return hb0.at[pl.ds(yp(k) * NX, NX)]

        def row_copy(from_k, to_k, sem):
            return copy(row(from_k), row(from_k), hs.at[sem], hr.at[yp(from_k) * NX], at_y(to_k), vo)

        def across(k):
            copy(row(k), row(k), hds.at[yp(k)], hdr.at[yp(k)], dp, sib).start()

        def row_got(k):
            got(row(k), hr.at[yp(k) * NX])

        row_copy(0, 1, 4).start()
        row_copy(0, -1, 5).start()
        row_copy(0, 4, 6).start()
        across(0)
        label_first()
        row_got(-1)
        row_copy(-1, 1, 7).start()
        row_got(1)
        row_copy(1, -1, 8).start()
        across(-1)
        across(1)
        label_second()
        row_got(4)
        row_copy(4, 1, 9).start()
        row_copy(4, -1, 10).start()
        across(4)
        for k in (2, -2, 3, -3):
            row_got(k)
            across(k)
        for k in (1, 2, 3):
            sent(hb0.at[dp], hs.at[k])
        for sem in range(4, 11):
            sent(row(0), hs.at[sem])

    @pl.when(c == 1)
    def _():
        hb1[dp] = hidden[:, SHARE:]

        def own(k):
            return hb1.at[at_y(k)]

        def spread(k):
            for i in (1, 2, 3):
                copy(own(k), own(k), hs.at[7 + yp(k) * 3 + i], hr.at[at_y(k)], yp(0) * NX + xp(i), vo).start()

        for k in (1, -1, 2, -2, 3, -3, 4):
            copy(own(0), own(0), hs.at[yp(k)], hr.at[dp], at_y(k), vo).start()
        spread(0)
        w_copy.wait()
        transpose_head(0, 18)
        for k in (1, -1):
            got(own(k), hr.at[at_y(k)])
            spread(k)
        label_first()
        for k in (2, -2, 3, -3, 4):
            got(own(k), hr.at[at_y(k)])
            spread(k)
        label_second()

        for k in (0, 1, -1, 2, -2, 3, -3, 4):
            for i in (1, 2, 3):
                slot = yp(k) * NX + xp(i)
                got(hb1.at[slot], hr.at[slot])
            rows = hb1.at[pl.ds(yp(k) * NX, NX)]
            copy(rows, rows, hds.at[yp(k)], hdr.at[yp(k)], dp, sib).start()
        for k in (1, -1, 2, -2, 3, -3, 4):
            sent(own(0), hs.at[yp(k)])
        for k in range(8, 32):
            sent(own(0), hs.at[k])

    for g in range(2):
        send_x(g, bpx, brx, bxs, bxr)
    def across_done(sending, arriving):
        def body(v, carry):
            got(arriving.at[pl.ds(v * NX, NX)], hdr.at[v])
            sent(sending.at[pl.ds(v * NX, NX)], hds.at[v])
            return carry

        lax.fori_loop(0, NY, body, 0)

    pl.when(c == 0)(lambda: across_done(hb0, hb1))
    pl.when(c == 1)(lambda: across_done(hb1, hb0))

    raw = jnp.zeros((ROWS, TOKENS), f32)
    for part, block in enumerate((hb0, hb1, hb1)):
        at = part * SHARE
        skip = max(at - SHARE, 0)
        h2[...] = block[:, :, skip:skip + SHARE].astype(f32).reshape(TOKENS, SHARE).astype(bf16)
        raw += lax.dot_general(
            wv[:, at:at + SHARE], h2[...], (((1,), (1,)), ((), ())), preferred_element_type=f32)
    squash = jnp.tanh(raw * (1.0 / softcap))
    terms = jnp.exp(softcap * squash)

    slope = 1.0 - squash * squash
    den_a[vo] = jnp.concatenate([
        jnp.sum(terms, axis=0, keepdims=True),
        jnp.sum(jnp.where(onehot, terms, 0.0), axis=0, keepdims=True),
        jnp.sum(jnp.where(onehot, slope, 0.0), axis=0, keepdims=True)], axis=1)
    each(LINE, lambda k: copy(
        den_a.at[vo], den_a.at[vo], das.at[k], dar.at[vo], dp, lax.rem(vo + k, LINE)).start())
    lt[0:ROWS, :] = jnp.where(onehot, 0.0, terms * slope).astype(bf16)
    for_sibling(lt, ds_, dr_, c_s, c_r)
    for g in range(2):
        own_half(g, lt, dr_, c_r, px, pz, rz, zs, zr)
        send_x(g, px, rx, xs, xr)
    each(LINE, lambda k: got(den_a.at[vo], dar.at[lax.rem(vo + k, LINE)]))
    each(LINE, lambda k: sent(den_a.at[vo], das.at[k]))
    den_b[dp] = jnp.sum(den_a[...], axis=0)
    each(PLANE, lambda k: copy(
        den_b.at[dp], den_b.at[dp], dbs.at[k], dbr.at[dp], lax.rem(dp + k, PLANE), vo).start())

    each(NZ, lambda k: got(brz.at[0], bzr.at[zp(k)]))
    label_z = bpz[z].astype(f32)
    for k in range(1, NZ):
        label_z += brz[zp(k)].astype(f32)
    bpz[z] = label_z.astype(bf16)
    for g in range(2):
        label_x = bpx[g, x].astype(f32)
        for k in (1, 2, 3):
            got(brx.at[g, 0], bxr.at[g, xp(k)])
            label_x += brx[g, xp(k)].astype(f32)
        bpx[g, x] = label_x.astype(bf16)

    each(PLANE, lambda k: got(den_b.at[dp], dbr.at[lax.rem(dp + k, PLANE)]))
    each(PLANE, lambda k: sent(den_b.at[dp], dbs.at[k]))
    sums = jnp.sum(den_b[...], axis=0)
    inverse = 1.0 / sums[:, 0:TOKENS]
    at_label = ((sums[:, TOKENS:2 * TOKENS] * inverse - 1.0) * sums[:, 2 * TOKENS:]).astype(bf16).astype(f32)

    each(NZ, lambda k: got(rz.at[0], zr.at[zp(k)]))
    total = pz[z].astype(f32)
    for k in range(1, NZ):
        total += rz[zp(k)].astype(f32)
    qz[...] = (total * inverse + bpz[z].astype(f32) * at_label).astype(bf16)
    for k in (1, 2, 3):
        copy(qz.at[xp(k)], r2z.at[x], z2s.at[k], z2r.at[x], at_x(k), vo).start()
    for g in range(2):
        total = px[g, x].astype(f32)
        for k in (1, 2, 3):
            got(rx.at[g, 0], xr.at[g, xp(k)])
            total += rx[g, xp(k)].astype(f32)
        qx[4 * g:4 * g + 4] = (total * inverse + bpx[g, x].astype(f32) * at_label).astype(bf16)
    each(NZ, lambda k: copy(
        qx.at[zp(k)], r2x.at[z], x2s.at[k], x2r.at[z], dp, at_z(k)).start())
    total = qz[x].astype(f32)
    for k in (1, 2, 3):
        got(r2z.at[0], z2r.at[xp(k)])
        total += r2z[xp(k)].astype(f32)
    ry[y, XU:] = total.astype(bf16)
    each(NZ, lambda k: got(r2x.at[0], x2r.at[zp(k)]))
    total = qx[z].astype(f32)
    for k in range(1, NZ):
        total += r2x[zp(k)].astype(f32)
    ry[y, 0:XU] = total.astype(bf16)

    each(NY, lambda k: copy(ry.at[y], ry.at[y], ys.at[k], yr.at[y], at_y(k), vo).start())
    each(NY, lambda k: got(ry.at[0], yr.at[yp(k)]))
    each(NY, lambda k: sent(ry.at[0], ys.at[k]))
    total = ry[0].astype(f32)
    for k in range(1, NY):
        total += ry[k].astype(f32)
    shift = lax.rem(z, 2) * 8 + c * 36

    def quarter(v):
        return gb.at[pl.ds(shift + v * UNITS, UNITS)]

    gb[pl.ds(shift + x * UNITS, UNITS)] = total.astype(bf16)

    @pl.when(holds)
    def _():
        def body(k, carry):
            @pl.when(jnp.logical_not(own_taker) | (k > 0))
            def _():
                copy(quarter(x), rb, bs.at[k], br, taker_dp, zp(k) * NC + taker_core).start()

            return carry

        lax.fori_loop(0, NZ, body, 0)

    for k in (1, 2, 3):
        copy(quarter(x), quarter(x), gs.at[k], gr.at[x], at_x(k), vo).start()
    copy(quarter(x), quarter(x), gds.at[x], gdr.at[x], dp, sib).start()

    @pl.when(holds & own_taker)
    def _():
        rb[...] = gb[pl.ds(shift + x * UNITS, UNITS)]

    for k in (1, 3, 2):
        got(quarter(xp(k)), gr.at[xp(k)])
        copy(quarter(xp(k)), quarter(xp(k)), gds.at[xp(k)], gdr.at[xp(k)], dp, sib).start()

    block = gb[pl.ds(shift, 36)].astype(f32).reshape(CHUNK, TOKENS).astype(bf16)
    token = lax.broadcasted_iota(jnp.int32, (8, TOKENS), 1)
    mine = jnp.where(token == dp * 8 + lax.broadcasted_iota(jnp.int32, (8, TOKENS), 0), 1.0, 0.0).astype(bf16)
    grads[...] = lax.dot_general(
        mine, block, (((1,), (1,)), ((), ())), preferred_element_type=f32).astype(bf16)
    new_factor[...] = decay_rate * factor[...]

    for v in range(NX):
        got(quarter(v), gdr.at[v])

    @pl.when(jnp.logical_not(holds & own_taker))
    def _():
        got(rb, br)

    rows = rb[...].astype(f32).reshape(72, TOKENS).astype(bf16)
    line_row = lax.broadcasted_iota(jnp.int32, (128, 72), 0)
    column = lax.broadcasted_iota(jnp.int32, (128, 72), 1)
    place, within = line_row // 16, lax.rem(line_row, 16)
    pick = jnp.where((within < 9) & (column == place * 9 + within), 1.0, 0.0).astype(bf16)
    spread_rows = jnp.dot(pick, rows, preferred_element_type=f32).astype(bf16)
    columns = gb[...].astype(f32).reshape(640, TOKENS).astype(bf16)
    gram = lax.dot_general(spread_rows, columns, (((1,), (1,)), ((), ())), preferred_element_type=f32)
    tb[...] = gram.reshape(NZ, 16, 640).astype(bf16)

    def to_place(k, carry):
        place = zp(k)

        @pl.when(NZ * c + place != vo)
        def _():
            copy(tb.at[place], rt.at[z], ts.at[place], tr.at[z], dp, NZ * c + place).start()

        return carry

    lax.fori_loop(0, NZ, to_place, 0)
    sender = z // 4

    @pl.when(sender == c)
    def _():
        rt[z] = tb[lax.rem(vo, NZ)]

    scale = (1.0 - decay_rate) * (D / TOKENS)
    for v in range(NZ):
        @pl.when(v * NC + sender != vo)
        def _():
            got(rt.at[0], tr.at[v])

        at = v * NC * CHUNK // 128 * 128
        new_factor[:, at:at + 640] += scale * rt[v].astype(f32)[0:9]

    def places_sent(place, carry):
        @pl.when(NZ * c + place != vo)
        def _():
            sent(tb.at[0], ts.at[place])

        @pl.when(holds & (jnp.logical_not(own_taker) | (place > 0)))
        def _():
            sent(rb, bs.at[place])

        return carry

    lax.fori_loop(0, NZ, places_sent, 0)
    for v in range(NX):
        sent(quarter(v), gds.at[v])
    for k in (1, 2, 3):
        sent(quarter(x), gs.at[k])

    each(NZ, lambda k: sent(pz.at[0], zs.at[zp(k)]))
    each(NZ, lambda k: sent(bpz.at[0], bzs.at[zp(k)]))
    each(NZ, lambda k: sent(qx.at[0], x2s.at[k]))
    for k in (1, 2, 3):
        sent(qz.at[0], z2s.at[k])
        for g in range(2):
            sent(px.at[g, 0], xs.at[g, k])
            sent(bpx.at[g, 0], bxs.at[g, k])
    lax.fori_loop(0, NZ, lambda i, carry: (sent(ds_.at[i], c_s.at[i]), sent(bds.at[i], bc_s.at[i]), carry)[2], 0)


def on_device(hidden, labels, head_weight, factor_rows):
    vmem = pl.BlockSpec(memory_space=pltpu.VMEM)
    dma = pltpu.SemaphoreType.DMA

    def buf(*shape, dtype=bf16):
        return pltpu.VMEM(shape, dtype)

    return pl.pallas_call(
        kernel,
        out_shape=(
            jax.ShapeDtypeStruct(factor_rows.shape, f32),
            jax.ShapeDtypeStruct((TOKENS // PLANE, CHUNK), bf16),
        ),
        in_specs=[vmem, vmem, pl.BlockSpec(memory_space=pl.ANY), vmem],
        out_specs=(vmem, vmem),
        scratch_shapes=[
            buf(ROWS, D), buf(D, PADDED), buf(PLANE, 8, SHARE), buf(PLANE, 8, D - SHARE), buf(TOKENS, SHARE), buf(PADDED, TOKENS),
            buf(NZ, NX, UNITS, 8, TOKENS), buf(NZ, NX, UNITS, 8, TOKENS),
            buf(2, NX, 4, XU, 8, TOKENS), buf(NZ, NX, UNITS - XU, 8, TOKENS),
            buf(2, NX, 4, XU, 8, TOKENS), buf(NZ, NX, UNITS - XU, 8, TOKENS),
            buf(NZ, XU, 8, TOKENS), buf(NX, UNITS - XU, 8, TOKENS),
            buf(NZ, XU, 8, TOKENS), buf(NX, UNITS - XU, 8, TOKENS),
            buf(NY, UNITS, 8, TOKENS), buf(80, 8, TOKENS), buf(UNITS, 8, TOKENS),
            buf(NZ, 16, 640), buf(NZ, 16, 640),
            buf(LINE, 1, 3 * TOKENS, dtype=f32), buf(PLANE, 1, 3 * TOKENS, dtype=f32), buf(PADDED, TOKENS),
            buf(NZ, NX, UNITS, 8, TOKENS), buf(NZ, NX, UNITS, 8, TOKENS),
            buf(2, NX, 4, XU, 8, TOKENS), buf(NZ, NX, UNITS - XU, 8, TOKENS),
            buf(2, NX, 4, XU, 8, TOKENS), buf(NZ, NX, UNITS - XU, 8, TOKENS),
            dma, dma((32,)), dma((32,)), dma((8,)), dma((8,)),
            dma((LINE,)), dma((LINE,)), dma((PLANE,)), dma((PLANE,)), dma((NZ,)), dma((NZ,)),
            dma((2, NX)), dma((2, NX)), dma((NZ,)), dma((NZ,)), dma((NZ,)), dma((NZ,)), dma((NX,)), dma((NX,)),
            dma((NY,)), dma((NY,)), dma((NX,)), dma((NX,)), dma((NZ,)), dma, dma((NZ,)), dma((NZ,)), dma((NX,)), dma((NX,)),
            dma((NZ,)), dma((NZ,)), dma((2, NX)), dma((2, NX)), dma((NZ,)), dma((NZ,)),
        ],
        compiler_params=pltpu.CompilerParams(
            collective_id=0, has_side_effects=True, vmem_limit_bytes=56 * 2**20),
        cost_estimate=pl.CostEstimate(flops=4 * 500 * 256 * 4608, bytes_accessed=6 * 2**20, transcendentals=2 * 500 * 256),
    )(hidden, labels.reshape(1, TOKENS), head_weight, factor_rows)


def solution(mesh):
    placed = (P("dp", None), P(), P(("dp", "vocab"), None), P(("dp", "vocab"), None))
    return jax.shard_map(
        on_device,
        mesh=mesh,
        in_specs=placed,
        out_specs=(P(("dp", "vocab"), None), P("dp", "vocab")),
        check_vma=False,
    )
```

```python
import jax
import jax.numpy as jnp
from jax import lax
from jax.experimental import pallas as pl
from jax.experimental.pallas import tpu as pltpu
from jax.sharding import PartitionSpec as P

softcap = 30.0
decay_rate = 0.95

NX, NY, NZ, NC = 4, 8, 8, 2
PLANE, LINE = NX * NY, NZ * NC
D, TOKENS, ROWS = 4608, 256, 500
PADDED = 512
SHARE = D // 3
CHUNK = D // LINE
UNITS = CHUNK // 8 // NX
XU = 6
MESH = pl.DeviceIdType.MESH
f32, bf16 = jnp.float32, jnp.bfloat16


def kernel(
    hidden_in, labels_in, head, gram_rows, grads,
    hidden, labels, wv, wt, hb0, hb1, h2, lt, ds_, dr_, px, pz, rx, rz, qx, qz, r2x, r2z, ry, gb, rb, tb, rt, den_a, den_b, lab, bds, bdr, bpx, bpz, brx, brz,
    w_sem, in_sem, hs, hr, hds, hdr, das, dar, dbs, dbr, c_s, c_r, xs, xr, zs, zr, x2s, x2r, z2s, z2r,
    ys, yr, gs, gr, bs, br, ts, tr, gds, gdr, bc_s, bc_r, bxs, bxr, bzs, bzr,
):
    dp, vo = lax.axis_index("dp"), lax.axis_index("vocab")
    x, y = lax.rem(dp, NX), dp // NX
    c, z = lax.rem(vo, NC), vo // NC
    sib = vo + 1 - 2 * c

    def copy(src, dst, send, recv, to_dp, to_vo):
        return pltpu.make_async_remote_copy(
            src_ref=src, dst_ref=dst, send_sem=send, recv_sem=recv, device_id=(to_dp, to_vo), device_id_type=MESH
        )

    def got(ref, recv):
        copy(ref, ref, recv, recv, dp, sib).wait_recv()

    def sent(ref, send):
        copy(ref, ref, send, send, dp, sib).wait_send()

    def each(count, body):
        lax.fori_loop(1, count, lambda k, carry: (body(k), carry)[1], 0)

    def xp(k):
        return lax.rem(x + k, NX)

    def yp(k):
        return lax.rem(y + k + NY, NY)

    def zp(k):
        return lax.rem(z + k, NZ)

    def at_x(k):
        return y * NX + xp(k)

    def at_y(k):
        return yp(k) * NX + x

    def at_z(k):
        return zp(k) * NC + c

    w_copy = pltpu.make_async_copy(head, wv, w_sem)
    hidden_copy = pltpu.make_async_copy(hidden_in, hidden, in_sem.at[0])
    labels_copy = pltpu.make_async_copy(labels_in, labels, in_sem.at[1])
    hidden_copy.start()
    labels_copy.start()
    w_copy.start()
    gb[...] = jnp.zeros_like(gb)

    barrier = pltpu.get_barrier_semaphore()
    each(LINE, lambda k: pl.semaphore_signal(
        barrier, inc=1, device_id=(dp, lax.rem(vo + k, LINE)), device_id_type=MESH))
    each(PLANE, lambda k: pl.semaphore_signal(
        barrier, inc=1, device_id=(lax.rem(dp + k, PLANE), vo), device_id_type=MESH))
    wt[:, PADDED - 128:] = jnp.zeros((D, 128), bf16)
    lt[PADDED - 16:, :] = jnp.zeros((16, TOKENS), bf16)
    lab[PADDED - 16:, :] = jnp.zeros((16, TOKENS), bf16)
    pl.semaphore_wait(barrier, LINE + PLANE - 2)
    hidden_copy.wait()
    labels_copy.wait()

    def transpose_head(first, last):
        def body(b, carry):
            at = pl.multiple_of(b * 256, 256)
            wt[pl.ds(at, 256), 0:ROWS] = wv[:, pl.ds(at, 256)].T
            return carry

        lax.fori_loop(first, last, body, 0)

    def partial_of(rows, i, core):
        start = pl.multiple_of((i * NC + core) * CHUNK, 32)
        product = jnp.dot(wt[pl.ds(start, CHUNK), :], rows[...], preferred_element_type=f32)
        return product.reshape(NX, UNITS, 8, TOKENS)

    def for_sibling(rows, out, arriving, s_sem, r_sem):
        def body(i, carry):
            out[i] = partial_of(rows, i, 1 - c).astype(bf16)
            copy(out.at[i], arriving.at[i], s_sem.at[i], r_sem.at[i], dp, sib).start()
            return carry

        lax.fori_loop(0, NZ, body, 0)

    def own_half(g, rows, arriving, r_sem, by_x, by_z, z_arriving, zs_sem, zr_sem):
        def body(i, carry):
            total = partial_of(rows, i, c)
            got(arriving.at[i], r_sem.at[i])
            total = (total + arriving[i].astype(f32)).astype(bf16)
            for v in range(NX):
                by_x[g, v, i - 4 * g] = total[v, 0:XU]
                by_z[i, v] = total[v, XU:]

            @pl.when(i != z)
            def _():
                copy(by_z.at[i], z_arriving.at[z], zs_sem.at[i], zr_sem.at[z], dp, i * NC + c).start()

            return carry

        lax.fori_loop(4 * g, 4 * g + 4, body, 0)

    def send_x(g, by_x, arriving, s_sem, r_sem):
        for k in (1, 2, 3):
            copy(by_x.at[g, xp(k)], arriving.at[g, x], s_sem.at[g, k], r_sem.at[g, x], at_x(k), vo).start()

    onehot = lax.broadcasted_iota(jnp.int32, (ROWS, TOKENS), 0) == labels[...] - (dp * LINE + vo) * ROWS

    def label_first():
        lab[0:ROWS, :] = onehot.astype(f32).astype(bf16)
        for_sibling(lab, bds, bdr, bc_s, bc_r)

    def label_second():
        for g in range(2):
            own_half(g, lab, bdr, bc_r, bpx, bpz, brz, bzs, bzr)

    @pl.when(c == 0)
    def _():
        hb0[dp] = hidden[:, 0:SHARE]
        for k in (1, 2, 3):
            copy(hb0.at[dp], hb0.at[dp], hs.at[k], hr.at[dp], at_x(k), vo).start()
        w_copy.wait()
        transpose_head(0, 18)
        for k in (1, 2, 3):
            got(hb0.at[at_x(k)], hr.at[at_x(k)])

        def row(k):
            return hb0.at[pl.ds(yp(k) * NX, NX)]

        def row_copy(from_k, to_k, sem):
            return copy(row(from_k), row(from_k), hs.at[sem], hr.at[yp(from_k) * NX], at_y(to_k), vo)

        def across(k):
            copy(row(k), row(k), hds.at[yp(k)], hdr.at[yp(k)], dp, sib).start()

        def row_got(k):
            got(row(k), hr.at[yp(k) * NX])

        row_copy(0, 1, 4).start()
        row_copy(0, -1, 5).start()
        row_copy(0, 4, 6).start()
        across(0)
        label_first()
        row_got(-1)
        row_copy(-1, 1, 7).start()
        row_got(1)
        row_copy(1, -1, 8).start()
        across(-1)
        across(1)
        label_second()
        row_got(4)
        row_copy(4, 1, 9).start()
        row_copy(4, -1, 10).start()
        across(4)
        for k in (2, -2, 3, -3):
            row_got(k)
            across(k)
        for k in (1, 2, 3):
            sent(hb0.at[dp], hs.at[k])
        for sem in range(4, 11):
            sent(row(0), hs.at[sem])

    @pl.when(c == 1)
    def _():
        hb1[dp] = hidden[:, SHARE:]

        def own(k):
            return hb1.at[at_y(k)]

        def spread(k):
            for i in (1, 2, 3):
                copy(own(k), own(k), hs.at[7 + yp(k) * 3 + i], hr.at[at_y(k)], yp(0) * NX + xp(i), vo).start()

        for k in (1, -1, 2, -2, 3, -3, 4):
            copy(own(0), own(0), hs.at[yp(k)], hr.at[dp], at_y(k), vo).start()
        spread(0)
        w_copy.wait()
        transpose_head(0, 18)
        for k in (1, -1):
            got(own(k), hr.at[at_y(k)])
            spread(k)
        label_first()
        for k in (2, -2, 3, -3, 4):
            got(own(k), hr.at[at_y(k)])
            spread(k)
        label_second()

        for k in (0, 1, -1, 2, -2, 3, -3, 4):
            for i in (1, 2, 3):
                slot = yp(k) * NX + xp(i)
                got(hb1.at[slot], hr.at[slot])
            rows = hb1.at[pl.ds(yp(k) * NX, NX)]
            copy(rows, rows, hds.at[yp(k)], hdr.at[yp(k)], dp, sib).start()
        for k in (1, -1, 2, -2, 3, -3, 4):
            sent(own(0), hs.at[yp(k)])
        for k in range(8, 32):
            sent(own(0), hs.at[k])

    for g in range(2):
        send_x(g, bpx, brx, bxs, bxr)
    def across_done(sending, arriving):
        def body(v, carry):
            got(arriving.at[pl.ds(v * NX, NX)], hdr.at[v])
            sent(sending.at[pl.ds(v * NX, NX)], hds.at[v])
            return carry

        lax.fori_loop(0, NY, body, 0)

    pl.when(c == 0)(lambda: across_done(hb0, hb1))
    pl.when(c == 1)(lambda: across_done(hb1, hb0))

    raw = jnp.zeros((ROWS, TOKENS), f32)
    for part, block in enumerate((hb0, hb1, hb1)):
        at = part * SHARE
        skip = max(at - SHARE, 0)
        h2[...] = block[:, :, skip:skip + SHARE].astype(f32).reshape(TOKENS, SHARE).astype(bf16)
        raw += lax.dot_general(
            wv[:, at:at + SHARE], h2[...], (((1,), (1,)), ((), ())), preferred_element_type=f32)
    squash = jnp.tanh(raw * (1.0 / softcap))
    terms = jnp.exp(softcap * squash)

    slope = 1.0 - squash * squash
    den_a[vo] = jnp.concatenate([
        jnp.sum(terms, axis=0, keepdims=True),
        jnp.sum(jnp.where(onehot, terms, 0.0), axis=0, keepdims=True),
        jnp.sum(jnp.where(onehot, slope, 0.0), axis=0, keepdims=True)], axis=1)
    each(LINE, lambda k: copy(
        den_a.at[vo], den_a.at[vo], das.at[k], dar.at[vo], dp, lax.rem(vo + k, LINE)).start())
    lt[0:ROWS, :] = jnp.where(onehot, 0.0, terms * slope).astype(bf16)
    for_sibling(lt, ds_, dr_, c_s, c_r)
    for g in range(2):
        own_half(g, lt, dr_, c_r, px, pz, rz, zs, zr)
        send_x(g, px, rx, xs, xr)
    each(LINE, lambda k: got(den_a.at[vo], dar.at[lax.rem(vo + k, LINE)]))
    each(LINE, lambda k: sent(den_a.at[vo], das.at[k]))
    den_b[dp] = jnp.sum(den_a[...], axis=0)
    each(PLANE, lambda k: copy(
        den_b.at[dp], den_b.at[dp], dbs.at[k], dbr.at[dp], lax.rem(dp + k, PLANE), vo).start())

    each(NZ, lambda k: got(brz.at[0], bzr.at[zp(k)]))
    label_z = bpz[z].astype(f32)
    for k in range(1, NZ):
        label_z += brz[zp(k)].astype(f32)
    bpz[z] = label_z.astype(bf16)
    for g in range(2):
        label_x = bpx[g, x].astype(f32)
        for k in (1, 2, 3):
            got(brx.at[g, 0], bxr.at[g, xp(k)])
            label_x += brx[g, xp(k)].astype(f32)
        bpx[g, x] = label_x.astype(bf16)

    each(PLANE, lambda k: got(den_b.at[dp], dbr.at[lax.rem(dp + k, PLANE)]))
    each(PLANE, lambda k: sent(den_b.at[dp], dbs.at[k]))
    sums = jnp.sum(den_b[...], axis=0)
    inverse = 1.0 / sums[:, 0:TOKENS]
    at_label = ((sums[:, TOKENS:2 * TOKENS] * inverse - 1.0) * sums[:, 2 * TOKENS:]).astype(bf16).astype(f32)

    each(NZ, lambda k: got(rz.at[0], zr.at[zp(k)]))
    total = pz[z].astype(f32)
    for k in range(1, NZ):
        total += rz[zp(k)].astype(f32)
    qz[...] = (total * inverse + bpz[z].astype(f32) * at_label).astype(bf16)
    for k in (1, 2, 3):
        copy(qz.at[xp(k)], r2z.at[x], z2s.at[k], z2r.at[x], at_x(k), vo).start()
    for g in range(2):
        total = px[g, x].astype(f32)
        for k in (1, 2, 3):
            got(rx.at[g, 0], xr.at[g, xp(k)])
            total += rx[g, xp(k)].astype(f32)
        qx[4 * g:4 * g + 4] = (total * inverse + bpx[g, x].astype(f32) * at_label).astype(bf16)
    each(NZ, lambda k: copy(
        qx.at[zp(k)], r2x.at[z], x2s.at[k], x2r.at[z], dp, at_z(k)).start())
    total = qz[x].astype(f32)
    for k in (1, 2, 3):
        got(r2z.at[0], z2r.at[xp(k)])
        total += r2z[xp(k)].astype(f32)
    ry[y, XU:] = total.astype(bf16)
    each(NZ, lambda k: got(r2x.at[0], x2r.at[zp(k)]))
    total = qx[z].astype(f32)
    for k in range(1, NZ):
        total += r2x[zp(k)].astype(f32)
    ry[y, 0:XU] = total.astype(bf16)

    each(NY, lambda k: copy(ry.at[y], ry.at[y], ys.at[k], yr.at[y], at_y(k), vo).start())
    each(NY, lambda k: got(ry.at[0], yr.at[yp(k)]))
    each(NY, lambda k: sent(ry.at[0], ys.at[k]))
    total = ry[0].astype(f32)
    for k in range(1, NY):
        total += ry[k].astype(f32)
    taker_dp, taker_core = y * NX + 2 * c + x // 2, lax.rem(x, 2)
    holds = z == y
    own_taker = (taker_dp == dp) & (taker_core == c)
    shift = lax.rem(z, 2) * 8 + c * 36

    def quarter(v):
        return gb.at[pl.ds(shift + v * UNITS, UNITS)]

    gb[pl.ds(shift + x * UNITS, UNITS)] = total.astype(bf16)

    @pl.when(holds)
    def _():
        def body(k, carry):
            @pl.when(jnp.logical_not(own_taker) | (k > 0))
            def _():
                copy(quarter(x), rb, bs.at[k], br, taker_dp, zp(k) * NC + taker_core).start()

            return carry

        lax.fori_loop(0, NZ, body, 0)

    for k in (1, 2, 3):
        copy(quarter(x), quarter(x), gs.at[k], gr.at[x], at_x(k), vo).start()
    copy(quarter(x), quarter(x), gds.at[x], gdr.at[x], dp, sib).start()

    @pl.when(holds & own_taker)
    def _():
        rb[...] = gb[pl.ds(shift + x * UNITS, UNITS)]

    for k in (1, 3, 2):
        got(quarter(xp(k)), gr.at[xp(k)])
        copy(quarter(xp(k)), quarter(xp(k)), gds.at[xp(k)], gdr.at[xp(k)], dp, sib).start()

    block = gb[pl.ds(shift, 36)].astype(f32).reshape(CHUNK, TOKENS).astype(bf16)
    token = lax.broadcasted_iota(jnp.int32, (8, TOKENS), 1)
    mine = jnp.where(token == dp * 8 + lax.broadcasted_iota(jnp.int32, (8, TOKENS), 0), 1.0, 0.0).astype(bf16)
    grads[...] = lax.dot_general(
        mine, block, (((1,), (1,)), ((), ())), preferred_element_type=f32).astype(bf16)
    gram_rows[...] = jnp.zeros_like(gram_rows)

    for v in range(NX):
        got(quarter(v), gdr.at[v])

    @pl.when(jnp.logical_not(holds & own_taker))
    def _():
        got(rb, br)

    rows = rb[...].astype(f32).reshape(72, TOKENS).astype(bf16)
    line_row = lax.broadcasted_iota(jnp.int32, (128, 72), 0)
    column = lax.broadcasted_iota(jnp.int32, (128, 72), 1)
    place, within = line_row // 16, lax.rem(line_row, 16)
    pick = jnp.where((within < 9) & (column == place * 9 + within), 1.0, 0.0).astype(bf16)
    spread_rows = jnp.dot(pick, rows, preferred_element_type=f32).astype(bf16)
    columns = gb[...].astype(f32).reshape(640, TOKENS).astype(bf16)
    gram = lax.dot_general(spread_rows, columns, (((1,), (1,)), ((), ())), preferred_element_type=f32)
    tb[...] = gram.reshape(NZ, 16, 640).astype(bf16)

    def to_place(k, carry):
        place = zp(k)

        @pl.when(NZ * c + place != vo)
        def _():
            copy(tb.at[place], rt.at[z], ts.at[place], tr.at[z], dp, NZ * c + place).start()

        return carry

    lax.fori_loop(0, NZ, to_place, 0)
    sender = z // 4

    @pl.when(sender == c)
    def _():
        rt[z] = tb[lax.rem(vo, NZ)]

    for v in range(NZ):
        @pl.when(v * NC + sender != vo)
        def _():
            got(rt.at[0], tr.at[v])

        at = v * NC * CHUNK // 128 * 128
        gram_rows[:, at:at + 640] += rt[v].astype(f32)[0:9]

    def places_sent(place, carry):
        @pl.when(NZ * c + place != vo)
        def _():
            sent(tb.at[0], ts.at[place])

        @pl.when(holds & (jnp.logical_not(own_taker) | (place > 0)))
        def _():
            sent(rb, bs.at[place])

        return carry

    lax.fori_loop(0, NZ, places_sent, 0)
    for v in range(NX):
        sent(quarter(v), gds.at[v])
    for k in (1, 2, 3):
        sent(quarter(x), gs.at[k])

    each(NZ, lambda k: sent(pz.at[0], zs.at[zp(k)]))
    each(NZ, lambda k: sent(bpz.at[0], bzs.at[zp(k)]))
    each(NZ, lambda k: sent(qx.at[0], x2s.at[k]))
    for k in (1, 2, 3):
        sent(qz.at[0], z2s.at[k])
        for g in range(2):
            sent(px.at[g, 0], xs.at[g, k])
            sent(bpx.at[g, 0], bxs.at[g, k])
    lax.fori_loop(0, NZ, lambda i, carry: (sent(ds_.at[i], c_s.at[i]), sent(bds.at[i], bc_s.at[i]), carry)[2], 0)


def update(gram_rows, grads_in, factor, new_factor, grads):
    scale = (1.0 - decay_rate) * (D / TOKENS)
    new_factor[...] = decay_rate * factor[...] + scale * gram_rows[...]
    grads[...] = grads_in[...]


def on_device(hidden, labels, head_weight, factor_rows):
    vmem = pl.BlockSpec(memory_space=pltpu.VMEM)
    dma = pltpu.SemaphoreType.DMA

    def buf(*shape, dtype=bf16):
        return pltpu.VMEM(shape, dtype)

    any_space = pl.BlockSpec(memory_space=pl.ANY)
    gram_rows, grads = pl.pallas_call(
        kernel,
        out_shape=(
            jax.ShapeDtypeStruct(factor_rows.shape, f32),
            jax.ShapeDtypeStruct((TOKENS // PLANE, CHUNK), bf16),
        ),
        in_specs=[any_space] * 3,
        out_specs=(vmem, vmem),
        scratch_shapes=[
            buf(TOKENS // PLANE, D), buf(1, TOKENS, dtype=jnp.int32), buf(ROWS, D), buf(D, PADDED), buf(PLANE, 8, SHARE), buf(PLANE, 8, D - SHARE), buf(TOKENS, SHARE), buf(PADDED, TOKENS),
            buf(NZ, NX, UNITS, 8, TOKENS), buf(NZ, NX, UNITS, 8, TOKENS),
            buf(2, NX, 4, XU, 8, TOKENS), buf(NZ, NX, UNITS - XU, 8, TOKENS),
            buf(2, NX, 4, XU, 8, TOKENS), buf(NZ, NX, UNITS - XU, 8, TOKENS),
            buf(NZ, XU, 8, TOKENS), buf(NX, UNITS - XU, 8, TOKENS),
            buf(NZ, XU, 8, TOKENS), buf(NX, UNITS - XU, 8, TOKENS),
            buf(NY, UNITS, 8, TOKENS), buf(80, 8, TOKENS), buf(UNITS, 8, TOKENS),
            buf(NZ, 16, 640), buf(NZ, 16, 640),
            buf(LINE, 1, 3 * TOKENS, dtype=f32), buf(PLANE, 1, 3 * TOKENS, dtype=f32), buf(PADDED, TOKENS),
            buf(NZ, NX, UNITS, 8, TOKENS), buf(NZ, NX, UNITS, 8, TOKENS),
            buf(2, NX, 4, XU, 8, TOKENS), buf(NZ, NX, UNITS - XU, 8, TOKENS),
            buf(2, NX, 4, XU, 8, TOKENS), buf(NZ, NX, UNITS - XU, 8, TOKENS),
            dma, dma((2,)), dma((32,)), dma((32,)), dma((8,)), dma((8,)),
            dma((LINE,)), dma((LINE,)), dma((PLANE,)), dma((PLANE,)), dma((NZ,)), dma((NZ,)),
            dma((2, NX)), dma((2, NX)), dma((NZ,)), dma((NZ,)), dma((NZ,)), dma((NZ,)), dma((NX,)), dma((NX,)),
            dma((NY,)), dma((NY,)), dma((NX,)), dma((NX,)), dma((NZ,)), dma, dma((NZ,)), dma((NZ,)), dma((NX,)), dma((NX,)),
            dma((NZ,)), dma((NZ,)), dma((2, NX)), dma((2, NX)), dma((NZ,)), dma((NZ,)),
        ],
        compiler_params=pltpu.CompilerParams(
            collective_id=0, has_side_effects=True, vmem_limit_bytes=56 * 2**20),
        cost_estimate=pl.CostEstimate(flops=4 * 500 * 256 * 4608, bytes_accessed=6 * 2**20, transcendentals=2 * 500 * 256),
    )(hidden, labels.reshape(1, TOKENS), head_weight)
    return pl.pallas_call(
        update,
        out_shape=(
            jax.ShapeDtypeStruct(factor_rows.shape, f32),
            jax.ShapeDtypeStruct(grads.shape, bf16),
        ),
        in_specs=[vmem] * 3,
        out_specs=(vmem, vmem),
    )(gram_rows, grads, factor_rows)


def solution(mesh):
    placed = (P("dp", None), P(), P(("dp", "vocab"), None), P(("dp", "vocab"), None))
    return jax.shard_map(
        on_device,
        mesh=mesh,
        in_specs=placed,
        out_specs=(P(("dp", "vocab"), None), P("dp", "vocab")),
        check_vma=False,
    )
```

```python
import jax
import jax.numpy as jnp
from jax import lax
from jax.experimental import pallas as pl
from jax.experimental.pallas import tpu as pltpu
from jax.sharding import PartitionSpec as P

softcap = 30.0
decay_rate = 0.95

NX, NY, NZ, NC = 4, 8, 8, 2
PLANE, LINE = NX * NY, NZ * NC
D, TOKENS, ROWS = 4608, 256, 500
PADDED = 512
SHARE = D // 4
CHUNK = D // LINE
UNITS = CHUNK // 8 // NX
XU, ZU, YU = 5, 2, 2
LXU, LZU = 2, 5
MESH = pl.DeviceIdType.MESH
f32, bf16 = jnp.float32, jnp.bfloat16


def kernel(
    hidden_in, labels_in, head, gram_rows, grads,
    hidden, labels, wv, wt, hb0, hb1, h2, lt, ds_, dr_, px, pz, rx, rz, qx, qz, r2x, r2z, ry, gb, rb, tb, rt, den_a, den_b, lab, bds, bdr, bpx, bpz, brx, brz,
    py, r1y, bpy, br1y, qy, r2y, sy, r3y, yb,
    bqx, bqz, bqy, br2x, br2z, br2y, label,
    w_sem, in_sem, hs, hr, hds, hdr, das, dar, dbs, dbr, c_s, c_r, xs, xr, zs, zr, x2s, x2r, z2s, z2r,
    ys, yr, gs, gr, bs, br, ts, tr, gds, gdr, bc_s, bc_r, bxs, bxr, bzs, bzr,
    y1s, y1r, by1s, by1r, y2s, y2r, y3s, y3r, y4s, y4r, bx2s, bx2r, bz2s, bz2r, by2s, by2r,
):
    dp, vo = lax.axis_index("dp"), lax.axis_index("vocab")
    x, y = lax.rem(dp, NX), dp // NX
    c, z = lax.rem(vo, NC), vo // NC
    sib = vo + 1 - 2 * c

    def copy(src, dst, send, recv, to_dp, to_vo):
        return pltpu.make_async_remote_copy(
            src_ref=src, dst_ref=dst, send_sem=send, recv_sem=recv, device_id=(to_dp, to_vo), device_id_type=MESH
        )

    def got(ref, recv):
        copy(ref, ref, recv, recv, dp, sib).wait_recv()

    def sent(ref, send):
        copy(ref, ref, send, send, dp, sib).wait_send()

    def each(count, body):
        lax.fori_loop(1, count, lambda k, carry: (body(k), carry)[1], 0)

    def xp(k):
        return lax.rem(x + k, NX)

    def yp(k):
        return lax.rem(y + k + NY, NY)

    def zp(k):
        return lax.rem(z + k, NZ)

    def at_x(k):
        return y * NX + xp(k)

    def at_y(k):
        return yp(k) * NX + x

    def at_z(k):
        return zp(k) * NC + c

    w_copy = pltpu.make_async_copy(head, wv, w_sem)
    hidden_copy = pltpu.make_async_copy(hidden_in, hidden, in_sem.at[0])
    labels_copy = pltpu.make_async_copy(labels_in, labels, in_sem.at[1])
    hidden_copy.start()
    labels_copy.start()
    w_copy.start()
    gb[...] = jnp.zeros_like(gb)

    barrier = pltpu.get_barrier_semaphore()
    each(LINE, lambda k: pl.semaphore_signal(
        barrier, inc=1, device_id=(dp, lax.rem(vo + k, LINE)), device_id_type=MESH))
    each(PLANE, lambda k: pl.semaphore_signal(
        barrier, inc=1, device_id=(lax.rem(dp + k, PLANE), vo), device_id_type=MESH))
    wt[:, PADDED - 128:] = jnp.zeros((D, 128), bf16)
    lt[PADDED - 16:, :] = jnp.zeros((16, TOKENS), bf16)
    lab[PADDED - 16:, :] = jnp.zeros((16, TOKENS), bf16)
    pl.semaphore_wait(barrier, LINE + PLANE - 2)
    hidden_copy.wait()
    labels_copy.wait()

    def transpose_head(first, last):
        def body(b, carry):
            at = pl.multiple_of(b * 256, 256)
            wt[pl.ds(at, 256), 0:ROWS] = wv[:, pl.ds(at, 256)].T
            return carry

        lax.fori_loop(first, last, body, 0)

    def partial_of(rows, i, core):
        start = pl.multiple_of((i * NC + core) * CHUNK, 32)
        product = jnp.dot(wt[pl.ds(start, CHUNK), :], rows[...], preferred_element_type=f32)
        return product.reshape(NX, UNITS, 8, TOKENS)

    def for_sibling(rows, out, arriving, s_sem, r_sem):
        def body(i, carry):
            out[i] = partial_of(rows, i, 1 - c).astype(bf16)
            copy(out.at[i], arriving.at[i], s_sem.at[i], r_sem.at[i], dp, sib).start()
            return carry

        lax.fori_loop(0, NZ, body, 0)

    def own_half(g, rows, arriving, r_sem, by_x, by_z, z_arriving, zs_sem, zr_sem, by_y, y_arriving, ys_sem, yr_sem):
        def body(i, carry):
            total = partial_of(rows, i, c)
            got(arriving.at[i], r_sem.at[i])
            total = (total + arriving[i].astype(f32)).astype(bf16)
            for v in range(NX):
                by_x[g, v, i - 4 * g] = total[v, 0:by_x.shape[3]]
                by_z[i, v] = total[v, by_x.shape[3]:XU + ZU]
                by_y[i, v] = total[v, XU + ZU:]

            @pl.when(i != z)
            def _():
                copy(by_z.at[i], z_arriving.at[z], zs_sem.at[i], zr_sem.at[z], dp, i * NC + c).start()

            @pl.when(i != y)
            def _():
                copy(by_y.at[i], y_arriving.at[y], ys_sem.at[i], yr_sem.at[y], i * NX + x, vo).start()

            return carry

        lax.fori_loop(4 * g, 4 * g + 4, body, 0)

    def send_x(g, by_x, arriving, s_sem, r_sem):
        for k in (1, 2, 3):
            copy(by_x.at[g, xp(k)], arriving.at[g, x], s_sem.at[g, k], r_sem.at[g, x], at_x(k), vo).start()

    onehot = lax.broadcasted_iota(jnp.int32, (ROWS, TOKENS), 0) == labels[...] - (dp * LINE + vo) * ROWS

    def label_first():
        lab[0:ROWS, :] = onehot.astype(f32).astype(bf16)
        for_sibling(lab, bds, bdr, bc_s, bc_r)

    def label_second():
        for g in range(2):
            own_half(g, lab, bdr, bc_r, bpx, bpz, brz, bzs, bzr, bpy, br1y, by1s, by1r)

    @pl.when(c == 0)
    def _():
        hb0[dp] = hidden[:, 0:SHARE]
        for k in (1, 2, 3):
            copy(hb0.at[dp], hb0.at[dp], hs.at[k], hr.at[dp], at_x(k), vo).start()
        w_copy.wait()
        transpose_head(0, 18)
        for k in (1, 2, 3):
            got(hb0.at[at_x(k)], hr.at[at_x(k)])

        def row(k):
            return hb0.at[pl.ds(yp(k) * NX, NX)]

        def row_copy(from_k, to_k, sem):
            return copy(row(from_k), row(from_k), hs.at[sem], hr.at[yp(from_k) * NX], at_y(to_k), vo)

        def across(k):
            copy(row(k), row(k), hds.at[yp(k)], hdr.at[yp(k)], dp, sib).start()

        def row_got(k):
            got(row(k), hr.at[yp(k) * NX])

        row_copy(0, 1, 4).start()
        row_copy(0, -1, 5).start()
        row_copy(0, 4, 6).start()
        across(0)
        label_first()
        row_got(-1)
        row_copy(-1, 1, 7).start()
        row_got(1)
        row_copy(1, -1, 8).start()
        across(-1)
        across(1)
        label_second()
        row_got(4)
        row_copy(4, 1, 9).start()
        row_copy(4, -1, 10).start()
        across(4)
        for k in (2, -2, 3, -3):
            row_got(k)
            across(k)
        for k in (1, 2, 3):
            sent(hb0.at[dp], hs.at[k])
        for sem in range(4, 11):
            sent(row(0), hs.at[sem])

    @pl.when(c == 1)
    def _():
        hb1[dp] = hidden[:, SHARE:]

        def own(k):
            return hb1.at[at_y(k)]

        def spread(k):
            for i in (1, 2, 3):
                copy(own(k), own(k), hs.at[7 + yp(k) * 3 + i], hr.at[at_y(k)], yp(0) * NX + xp(i), vo).start()

        for k in (1, -1, 2, -2, 3, -3, 4):
            copy(own(0), own(0), hs.at[yp(k)], hr.at[dp], at_y(k), vo).start()
        spread(0)
        w_copy.wait()
        transpose_head(0, 18)
        for k in (1, -1):
            got(own(k), hr.at[at_y(k)])
            spread(k)
        label_first()
        for k in (2, -2, 3, -3, 4):
            got(own(k), hr.at[at_y(k)])
            spread(k)
        label_second()

        for k in (0, 1, -1, 2, -2, 3, -3, 4):
            for i in (1, 2, 3):
                slot = yp(k) * NX + xp(i)
                got(hb1.at[slot], hr.at[slot])
            rows = hb1.at[pl.ds(yp(k) * NX, NX)]
            copy(rows, rows, hds.at[yp(k)], hdr.at[yp(k)], dp, sib).start()
        for k in (1, -1, 2, -2, 3, -3, 4):
            sent(own(0), hs.at[yp(k)])
        for k in range(8, 32):
            sent(own(0), hs.at[k])

    for g in range(2):
        send_x(g, bpx, brx, bxs, bxr)
    def across_done(sending, arriving):
        def body(v, carry):
            got(arriving.at[pl.ds(v * NX, NX)], hdr.at[v])
            sent(sending.at[pl.ds(v * NX, NX)], hds.at[v])
            return carry

        lax.fori_loop(0, NY, body, 0)

    pl.when(c == 0)(lambda: across_done(hb0, hb1))
    pl.when(c == 1)(lambda: across_done(hb1, hb0))

    raw = jnp.zeros((ROWS, TOKENS), f32)
    for part, block in enumerate((hb0, hb1, hb1, hb1)):
        at = part * SHARE
        skip = max(at - SHARE, 0)
        h2[...] = block[:, :, skip:skip + SHARE].astype(f32).reshape(TOKENS, SHARE).astype(bf16)
        raw += lax.dot_general(
            wv[:, at:at + SHARE], h2[...], (((1,), (1,)), ((), ())), preferred_element_type=f32)
    squash = jnp.tanh(raw * (1.0 / softcap))
    terms = jnp.exp(softcap * squash)

    slope = 1.0 - squash * squash
    den_a[vo] = jnp.concatenate([
        jnp.sum(terms, axis=0, keepdims=True),
        jnp.sum(jnp.where(onehot, terms, 0.0), axis=0, keepdims=True),
        jnp.sum(jnp.where(onehot, slope, 0.0), axis=0, keepdims=True)], axis=1)
    each(LINE, lambda k: copy(
        den_a.at[vo], den_a.at[vo], das.at[k], dar.at[vo], dp, lax.rem(vo + k, LINE)).start())
    lt[0:ROWS, :] = jnp.where(onehot, 0.0, terms * slope).astype(bf16)
    for_sibling(lt, ds_, dr_, c_s, c_r)
    for g in range(2):
        own_half(g, lt, dr_, c_r, px, pz, rz, zs, zr, py, r1y, y1s, y1r)
        send_x(g, px, rx, xs, xr)
    each(LINE, lambda k: got(den_a.at[vo], dar.at[lax.rem(vo + k, LINE)]))
    each(LINE, lambda k: sent(den_a.at[vo], das.at[k]))
    den_b[dp] = jnp.sum(den_a[...], axis=0)
    each(PLANE, lambda k: copy(
        den_b.at[dp], den_b.at[dp], dbs.at[k], dbr.at[dp], lax.rem(dp + k, PLANE), vo).start())

    def summed(own, arriving, count, at, recv):
        total = own.astype(f32)
        for k in range(1, count):
            got(arriving.at[0], recv.at[at(k)])
            total += arriving[at(k)].astype(f32)
        return total

    def x_sum(g, own, arriving, recv):
        total = own[g, x].astype(f32)
        for k in (1, 2, 3):
            got(arriving.at[g, 0], recv.at[g, xp(k)])
            total += arriving[g, xp(k)].astype(f32)
        return total.astype(bf16)

    def over_x(rows, arriving, s_sem, r_sem):
        for k in (1, 2, 3):
            copy(rows.at[xp(k)], arriving.at[x], s_sem.at[k], r_sem.at[x], at_x(k), vo).start()

    def over_z(g, rows, arriving, s_sem, r_sem):
        def body(i, carry):
            @pl.when(i != z)
            def _():
                copy(rows.at[i], arriving.at[z], s_sem.at[i], r_sem.at[z], dp, i * NC + c).start()

            return carry

        lax.fori_loop(4 * g, 4 * g + 4, body, 0)

    def second_step(by_x, by_z, by_y, rx_, rz_, ry_, xr_, zr_, yr_, qx_, qz_, qy_, r2x_, r2z_, r2y_,
                    x2s_, x2r_, z2s_, z2r_, y2s_, y2r_):
        qy_[...] = summed(by_y[y], ry_, NY, yp, yr_).astype(bf16)
        over_x(qy_, r2y_, y2s_, y2r_)
        qz_[...] = summed(by_z[z], rz_, NZ, zp, zr_).astype(bf16)
        over_x(qz_, r2z_, z2s_, z2r_)
        for g in range(2):
            qx_[4 * g:4 * g + 4] = x_sum(g, by_x, rx_, xr_)
            over_z(g, qx_, r2x_, x2s_, x2r_)

    second_step(bpx, bpz, bpy, brx, brz, br1y, bxr, bzr, by1r, bqx, bqz, bqy, br2x, br2z, br2y,
                bx2s, bx2r, bz2s, bz2r, by2s, by2r)
    second_step(px, pz, py, rx, rz, r1y, xr, zr, y1r, qx, qz, qy, r2x, r2z, r2y, x2s, x2r, z2s, z2r, y2s, y2r)
    label[XU + ZU:] = summed(bqy[x], br2y, NX, xp, by2r).astype(bf16)
    label[LXU:XU + ZU] = summed(bqz[x], br2z, NX, xp, bz2r).astype(bf16)
    label[0:LXU] = summed(bqx[z], br2x, NZ, zp, bx2r).astype(bf16)

    each(PLANE, lambda k: got(den_b.at[dp], dbr.at[lax.rem(dp + k, PLANE)]))
    each(PLANE, lambda k: sent(den_b.at[dp], dbs.at[k]))
    sums = jnp.sum(den_b[...], axis=0)
    inverse = 1.0 / sums[:, 0:TOKENS]
    at_label = ((sums[:, TOKENS:2 * TOKENS] * inverse - 1.0) * sums[:, 2 * TOKENS:]).astype(bf16).astype(f32)

    def joined(total, first, last):
        return (total * inverse + label[first:last].astype(f32) * at_label).astype(bf16)

    sy[...] = joined(summed(qy[x], r2y, NX, xp, y2r), XU + ZU, UNITS)

    @pl.when(z != y)
    def _():
        copy(sy, r3y.at[z], y3s, y3r.at[z], dp, y * NC + c).start()

    ry[y, XU:] = joined(summed(qz[x], r2z, NX, xp, z2r), XU, XU + ZU)
    ry[y, 0:XU] = joined(summed(qx[z], r2x, NZ, zp, x2r), 0, XU)

    each(NY, lambda k: copy(ry.at[y], ry.at[y], ys.at[k], yr.at[y], at_y(k), vo).start())

    @pl.when(z == y)
    def _():
        each(NZ, lambda k: got(r3y.at[0], y3r.at[zp(k)]))
        done = sy[...].astype(f32)
        for k in range(1, NZ):
            done += r3y[zp(k)].astype(f32)
        yb[...] = done.astype(bf16)
        each(NY, lambda k: copy(yb, yb, y4s.at[k], y4r, at_y(k), vo).start())

    each(NY, lambda k: got(ry.at[0], yr.at[yp(k)]))
    each(NY, lambda k: sent(ry.at[0], ys.at[k]))
    total = ry[0].astype(f32)
    for k in range(1, NY):
        total += ry[k].astype(f32)
    taker_dp, taker_core = y * NX + 2 * c + x // 2, lax.rem(x, 2)
    holds = z == y
    own_taker = (taker_dp == dp) & (taker_core == c)
    shift = lax.rem(z, 2) * 8 + c * 36

    def quarter(v):
        return gb.at[pl.ds(shift + v * UNITS, UNITS)]

    @pl.when(z != y)
    def _():
        got(yb, y4r)

    gb[pl.ds(shift + x * UNITS, XU + ZU)] = total.astype(bf16)
    gb[pl.ds(shift + x * UNITS + XU + ZU, YU)] = yb[...]

    @pl.when(holds)
    def _():
        def body(k, carry):
            @pl.when(jnp.logical_not(own_taker) | (k > 0))
            def _():
                copy(quarter(x), rb, bs.at[k], br, taker_dp, zp(k) * NC + taker_core).start()

            return carry

        lax.fori_loop(0, NZ, body, 0)

    for k in (1, 2, 3):
        copy(quarter(x), quarter(x), gs.at[k], gr.at[x], at_x(k), vo).start()
    copy(quarter(x), quarter(x), gds.at[x], gdr.at[x], dp, sib).start()

    @pl.when(holds & own_taker)
    def _():
        rb[...] = gb[pl.ds(shift + x * UNITS, UNITS)]

    for k in (1, 3, 2):
        got(quarter(xp(k)), gr.at[xp(k)])
        copy(quarter(xp(k)), quarter(xp(k)), gds.at[xp(k)], gdr.at[xp(k)], dp, sib).start()

    block = gb[pl.ds(shift, 36)].astype(f32).reshape(CHUNK, TOKENS).astype(bf16)
    token = lax.broadcasted_iota(jnp.int32, (8, TOKENS), 1)
    mine = jnp.where(token == dp * 8 + lax.broadcasted_iota(jnp.int32, (8, TOKENS), 0), 1.0, 0.0).astype(bf16)
    grads[...] = lax.dot_general(
        mine, block, (((1,), (1,)), ((), ())), preferred_element_type=f32).astype(bf16)
    gram_rows[...] = jnp.zeros_like(gram_rows)

    for v in range(NX):
        got(quarter(v), gdr.at[v])

    @pl.when(jnp.logical_not(holds & own_taker))
    def _():
        got(rb, br)

    rows = rb[...].astype(f32).reshape(72, TOKENS).astype(bf16)
    line_row = lax.broadcasted_iota(jnp.int32, (128, 72), 0)
    column = lax.broadcasted_iota(jnp.int32, (128, 72), 1)
    place, within = line_row // 16, lax.rem(line_row, 16)
    pick = jnp.where((within < 9) & (column == place * 9 + within), 1.0, 0.0).astype(bf16)
    spread_rows = jnp.dot(pick, rows, preferred_element_type=f32).astype(bf16)
    columns = gb[...].astype(f32).reshape(640, TOKENS).astype(bf16)
    gram = lax.dot_general(spread_rows, columns, (((1,), (1,)), ((), ())), preferred_element_type=f32)
    tb[...] = gram.reshape(NZ, 16, 640).astype(bf16)

    def to_place(k, carry):
        place = zp(k)

        @pl.when(NZ * c + place != vo)
        def _():
            copy(tb.at[place], rt.at[z], ts.at[place], tr.at[z], dp, NZ * c + place).start()

        return carry

    lax.fori_loop(0, NZ, to_place, 0)
    sender = z // 4

    @pl.when(sender == c)
    def _():
        rt[z] = tb[lax.rem(vo, NZ)]

    for v in range(NZ):
        @pl.when(v * NC + sender != vo)
        def _():
            got(rt.at[0], tr.at[v])

        at = v * NC * CHUNK // 128 * 128
        gram_rows[:, at:at + 640] += rt[v].astype(f32)[0:9]

    def places_sent(place, carry):
        @pl.when(NZ * c + place != vo)
        def _():
            sent(tb.at[0], ts.at[place])

        @pl.when(holds & (jnp.logical_not(own_taker) | (place > 0)))
        def _():
            sent(rb, bs.at[place])

        return carry

    lax.fori_loop(0, NZ, places_sent, 0)
    for v in range(NX):
        sent(quarter(v), gds.at[v])
    for k in (1, 2, 3):
        sent(quarter(x), gs.at[k])

    @pl.when(z == y)
    def _():
        each(NY, lambda k: sent(yb, y4s.at[k]))

    @pl.when(z != y)
    def _():
        sent(sy, y3s)

    each(NY, lambda k: sent(py.at[0], y1s.at[yp(k)]))
    each(NY, lambda k: sent(bpy.at[0], by1s.at[yp(k)]))
    each(NZ, lambda k: sent(pz.at[0], zs.at[zp(k)]))
    each(NZ, lambda k: sent(bpz.at[0], bzs.at[zp(k)]))
    each(NZ, lambda k: sent(qx.at[0], x2s.at[zp(k)]))
    each(NZ, lambda k: sent(bqx.at[0], bx2s.at[zp(k)]))
    for k in (1, 2, 3):
        sent(qz.at[0], z2s.at[k])
        sent(qy.at[0], y2s.at[k])
        sent(bqz.at[0], bz2s.at[k])
        sent(bqy.at[0], by2s.at[k])
        for g in range(2):
            sent(px.at[g, 0], xs.at[g, k])
            sent(bpx.at[g, 0], bxs.at[g, k])
    lax.fori_loop(0, NZ, lambda i, carry: (sent(ds_.at[i], c_s.at[i]), sent(bds.at[i], bc_s.at[i]), carry)[2], 0)


def update(gram_rows, grads_in, factor, new_factor, grads):
    scale = (1.0 - decay_rate) * (D / TOKENS)
    new_factor[...] = decay_rate * factor[...] + scale * gram_rows[...]
    grads[...] = grads_in[...]


def on_device(hidden, labels, head_weight, factor_rows):
    vmem = pl.BlockSpec(memory_space=pltpu.VMEM)
    dma = pltpu.SemaphoreType.DMA

    def buf(*shape, dtype=bf16):
        return pltpu.VMEM(shape, dtype)

    any_space = pl.BlockSpec(memory_space=pl.ANY)
    gram_rows, grads = pl.pallas_call(
        kernel,
        out_shape=(
            jax.ShapeDtypeStruct(factor_rows.shape, f32),
            jax.ShapeDtypeStruct((TOKENS // PLANE, CHUNK), bf16),
        ),
        in_specs=[any_space] * 3,
        out_specs=(vmem, vmem),
        scratch_shapes=[
            buf(TOKENS // PLANE, D), buf(1, TOKENS, dtype=jnp.int32), buf(ROWS, D), buf(D, PADDED), buf(PLANE, 8, SHARE), buf(PLANE, 8, D - SHARE), buf(TOKENS, SHARE), buf(PADDED, TOKENS),
            buf(NZ, NX, UNITS, 8, TOKENS), buf(NZ, NX, UNITS, 8, TOKENS),
            buf(2, NX, 4, XU, 8, TOKENS), buf(NZ, NX, ZU, 8, TOKENS),
            buf(2, NX, 4, XU, 8, TOKENS), buf(NZ, NX, ZU, 8, TOKENS),
            buf(NZ, XU, 8, TOKENS), buf(NX, ZU, 8, TOKENS),
            buf(NZ, XU, 8, TOKENS), buf(NX, ZU, 8, TOKENS),
            buf(NY, XU + ZU, 8, TOKENS), buf(80, 8, TOKENS), buf(UNITS, 8, TOKENS),
            buf(NZ, 16, 640), buf(NZ, 16, 640),
            buf(LINE, 1, 3 * TOKENS, dtype=f32), buf(PLANE, 1, 3 * TOKENS, dtype=f32), buf(PADDED, TOKENS),
            buf(NZ, NX, UNITS, 8, TOKENS), buf(NZ, NX, UNITS, 8, TOKENS),
            buf(2, NX, 4, LXU, 8, TOKENS), buf(NZ, NX, LZU, 8, TOKENS),
            buf(2, NX, 4, LXU, 8, TOKENS), buf(NZ, NX, LZU, 8, TOKENS),
            buf(NY, NX, YU, 8, TOKENS), buf(NY, NX, YU, 8, TOKENS), buf(NY, NX, YU, 8, TOKENS), buf(NY, NX, YU, 8, TOKENS),
            buf(NX, YU, 8, TOKENS), buf(NX, YU, 8, TOKENS), buf(YU, 8, TOKENS), buf(NZ, YU, 8, TOKENS),
            buf(YU, 8, TOKENS),
            buf(NZ, LXU, 8, TOKENS), buf(NX, LZU, 8, TOKENS), buf(NX, YU, 8, TOKENS),
            buf(NZ, LXU, 8, TOKENS), buf(NX, LZU, 8, TOKENS), buf(NX, YU, 8, TOKENS), buf(UNITS, 8, TOKENS),
            dma, dma((2,)), dma((32,)), dma((32,)), dma((8,)), dma((8,)),
            dma((LINE,)), dma((LINE,)), dma((PLANE,)), dma((PLANE,)), dma((NZ,)), dma((NZ,)),
            dma((2, NX)), dma((2, NX)), dma((NZ,)), dma((NZ,)), dma((NZ,)), dma((NZ,)), dma((NX,)), dma((NX,)),
            dma((NY,)), dma((NY,)), dma((NX,)), dma((NX,)), dma((NZ,)), dma, dma((NZ,)), dma((NZ,)), dma((NX,)), dma((NX,)),
            dma((NZ,)), dma((NZ,)), dma((2, NX)), dma((2, NX)), dma((NZ,)), dma((NZ,)),
            dma((NY,)), dma((NY,)), dma((NY,)), dma((NY,)), dma((NX,)), dma((NX,)), dma, dma((NZ,)), dma((NY,)), dma,
            dma((NZ,)), dma((NZ,)), dma((NX,)), dma((NX,)), dma((NX,)), dma((NX,)),
        ],
        compiler_params=pltpu.CompilerParams(
            collective_id=0, has_side_effects=True, vmem_limit_bytes=56 * 2**20),
        cost_estimate=pl.CostEstimate(flops=4 * 500 * 256 * 4608, bytes_accessed=6 * 2**20, transcendentals=2 * 500 * 256),
    )(hidden, labels.reshape(1, TOKENS), head_weight)
    return pl.pallas_call(
        update,
        out_shape=(
            jax.ShapeDtypeStruct(factor_rows.shape, f32),
            jax.ShapeDtypeStruct(grads.shape, bf16),
        ),
        in_specs=[vmem] * 3,
        out_specs=(vmem, vmem),
    )(gram_rows, grads, factor_rows)


def solution(mesh):
    placed = (P("dp", None), P(), P(("dp", "vocab"), None), P(("dp", "vocab"), None))
    return jax.shard_map(
        on_device,
        mesh=mesh,
        in_specs=placed,
        out_specs=(P(("dp", "vocab"), None), P("dp", "vocab")),
        check_vma=False,
    )
```

```python
import jax
import jax.numpy as jnp
from jax import lax
from jax.experimental import pallas as pl
from jax.experimental.pallas import tpu as pltpu
from jax.sharding import PartitionSpec as P

softcap = 30.0
decay_rate = 0.95

NX, NY, NZ, NC = 4, 8, 8, 2
PLANE, LINE = NX * NY, NZ * NC
D, TOKENS, ROWS = 4608, 256, 500
PADDED = 512
SHARE = D // 4
CHUNK = D // LINE
UNITS = CHUNK // 8 // NX
XU, ZU, YU = 5, 2, 2
LXU, LZU = 2, 5
MESH = pl.DeviceIdType.MESH
f32, bf16 = jnp.float32, jnp.bfloat16


def kernel(
    hidden_in, labels_in, head, gram_rows, grads,
    hidden, labels, wv, wt, hb0, hb1, h2, lt, ds_, dr_, px, pz, rx, rz, qx, qz, r2x, r2z, ry, gb, rb, tb, rt, den_a, den_b, lab, bds, bdr, bpx, bpz, brx, brz,
    py, r1y, bpy, br1y, qy, r2y, sy, r3y, yb,
    bqx, bqz, bqy, br2x, br2z, br2y, label,
    w_sem, in_sem, hs, hr, hds, hdr, das, dar, dbs, dbr, c_s, c_r, xs, xr, zs, zr, x2s, x2r, z2s, z2r,
    ys, yr, gs, gr, bs, br, ts, tr, gds, gdr, bc_s, bc_r, bxs, bxr, bzs, bzr,
    y1s, y1r, by1s, by1r, y2s, y2r, y3s, y3r, y4s, y4r, bx2s, bx2r, bz2s, bz2r, by2s, by2r,
):
    dp, vo = lax.axis_index("dp"), lax.axis_index("vocab")
    x, y = lax.rem(dp, NX), dp // NX
    c, z = lax.rem(vo, NC), vo // NC
    sib = vo + 1 - 2 * c

    def copy(src, dst, send, recv, to_dp, to_vo):
        return pltpu.make_async_remote_copy(
            src_ref=src, dst_ref=dst, send_sem=send, recv_sem=recv, device_id=(to_dp, to_vo), device_id_type=MESH
        )

    def got(ref, recv):
        copy(ref, ref, recv, recv, dp, sib).wait_recv()

    def sent(ref, send):
        copy(ref, ref, send, send, dp, sib).wait_send()

    def each(count, body):
        lax.fori_loop(1, count, lambda k, carry: (body(k), carry)[1], 0)

    def xp(k):
        return lax.rem(x + k, NX)

    def yp(k):
        return lax.rem(y + k + NY, NY)

    def zp(k):
        return lax.rem(z + k, NZ)

    def at_x(k):
        return y * NX + xp(k)

    def at_y(k):
        return yp(k) * NX + x

    def at_z(k):
        return zp(k) * NC + c

    w_copy = pltpu.make_async_copy(head, wv, w_sem)
    hidden_copy = pltpu.make_async_copy(hidden_in, hidden, in_sem.at[0])
    labels_copy = pltpu.make_async_copy(labels_in, labels, in_sem.at[1])
    hidden_copy.start()
    labels_copy.start()
    w_copy.start()
    gb[...] = jnp.zeros_like(gb)

    barrier = pltpu.get_barrier_semaphore()
    each(LINE, lambda k: pl.semaphore_signal(
        barrier, inc=1, device_id=(dp, lax.rem(vo + k, LINE)), device_id_type=MESH))
    each(PLANE, lambda k: pl.semaphore_signal(
        barrier, inc=1, device_id=(lax.rem(dp + k, PLANE), vo), device_id_type=MESH))
    wt[:, PADDED - 128:] = jnp.zeros((D, 128), bf16)
    lt[PADDED - 16:, :] = jnp.zeros((16, TOKENS), bf16)
    lab[PADDED - 16:, :] = jnp.zeros((16, TOKENS), bf16)
    pl.semaphore_wait(barrier, LINE + PLANE - 2)
    hidden_copy.wait()
    labels_copy.wait()

    def transpose_head(first, last):
        def body(b, carry):
            at = pl.multiple_of(b * 256, 256)
            wt[pl.ds(at, 256), 0:ROWS] = wv[:, pl.ds(at, 256)].T
            return carry

        lax.fori_loop(first, last, body, 0)

    def partial_of(rows, i, core):
        start = pl.multiple_of((i * NC + core) * CHUNK, 32)
        product = jnp.dot(wt[pl.ds(start, CHUNK), :], rows[...], preferred_element_type=f32)
        return product.reshape(NX, UNITS, 8, TOKENS)

    def for_sibling(rows, out, arriving, s_sem, r_sem):
        def body(i, carry):
            out[i] = partial_of(rows, i, 1 - c).astype(bf16)
            copy(out.at[i], arriving.at[i], s_sem, r_sem.at[i], dp, sib).start()
            return carry

        lax.fori_loop(0, NZ, body, 0)

    def own_half(g, rows, arriving, r_sem, by_x, by_z, z_arriving, zs_sem, zr_sem, by_y, y_arriving, ys_sem, yr_sem):
        def body(i, carry):
            total = partial_of(rows, i, c)
            got(arriving.at[i], r_sem.at[i])
            total = (total + arriving[i].astype(f32)).astype(bf16)
            for v in range(NX):
                by_x[g, v, i - 4 * g] = total[v, 0:by_x.shape[3]]
                by_z[i, v] = total[v, by_x.shape[3]:XU + ZU]
                by_y[i, v] = total[v, XU + ZU:]

            @pl.when(i != z)
            def _():
                copy(by_z.at[i], z_arriving.at[z], zs_sem, zr_sem, dp, i * NC + c).start()

            @pl.when(i != y)
            def _():
                copy(by_y.at[i], y_arriving.at[y], ys_sem, yr_sem, i * NX + x, vo).start()

            return carry

        lax.fori_loop(4 * g, 4 * g + 4, body, 0)

    def send_x(g, by_x, arriving, s_sem, r_sem):
        for k in (1, 2, 3):
            copy(by_x.at[g, xp(k)], arriving.at[g, x], s_sem, r_sem.at[g], at_x(k), vo).start()

    onehot = lax.broadcasted_iota(jnp.int32, (ROWS, TOKENS), 0) == labels[...] - (dp * LINE + vo) * ROWS

    def label_first():
        lab[0:ROWS, :] = onehot.astype(f32).astype(bf16)
        for_sibling(lab, bds, bdr, bc_s, bc_r)

    def label_second():
        for g in range(2):
            own_half(g, lab, bdr, bc_r, bpx, bpz, brz, bzs, bzr, bpy, br1y, by1s, by1r)

    @pl.when(c == 0)
    def _():
        hb0[dp] = hidden[:, 0:SHARE]
        for k in (1, 2, 3):
            copy(hb0.at[dp], hb0.at[dp], hs.at[0], hr.at[dp], at_x(k), vo).start()
        w_copy.wait()
        transpose_head(0, 18)
        for k in (1, 2, 3):
            got(hb0.at[at_x(k)], hr.at[at_x(k)])

        def row(k):
            return hb0.at[pl.ds(yp(k) * NX, NX)]

        def row_copy(from_k, to_k):
            return copy(row(from_k), row(from_k), hs.at[1], hr.at[yp(from_k) * NX], at_y(to_k), vo)

        def across(k):
            copy(row(k), row(k), hds, hdr, dp, sib).start()

        def row_got(k):
            got(row(k), hr.at[yp(k) * NX])

        row_copy(0, 1).start()
        row_copy(0, -1).start()
        row_copy(0, 4).start()
        across(0)
        label_first()
        row_got(-1)
        row_copy(-1, 1).start()
        row_got(1)
        row_copy(1, -1).start()
        across(-1)
        across(1)
        label_second()
        row_got(4)
        row_copy(4, 1).start()
        row_copy(4, -1).start()
        across(4)
        for k in (2, -2, 3, -3):
            row_got(k)
            across(k)
        sent(hb0.at[pl.ds(0, 3)], hs.at[0])
        sent(hb0.at[pl.ds(0, 28)], hs.at[1])

    @pl.when(c == 1)
    def _():
        hb1[dp] = hidden[:, SHARE:]

        def own(k):
            return hb1.at[at_y(k)]

        def spread(k):
            for i in (1, 2, 3):
                copy(own(k), own(k), hs.at[1], hr.at[at_y(k)], yp(0) * NX + xp(i), vo).start()

        for k in (1, -1, 2, -2, 3, -3, 4):
            copy(own(0), own(0), hs.at[0], hr.at[dp], at_y(k), vo).start()
        spread(0)
        w_copy.wait()
        transpose_head(0, 18)
        for k in (1, -1):
            got(own(k), hr.at[at_y(k)])
            spread(k)
        label_first()
        for k in (2, -2, 3, -3, 4):
            got(own(k), hr.at[at_y(k)])
            spread(k)
        label_second()

        for k in (0, 1, -1, 2, -2, 3, -3, 4):
            for i in (1, 2, 3):
                slot = yp(k) * NX + xp(i)
                got(hb1.at[slot], hr.at[slot])
            rows = hb1.at[pl.ds(yp(k) * NX, NX)]
            copy(rows, rows, hds, hdr, dp, sib).start()
        sent(hb1.at[pl.ds(0, 7)], hs.at[0])
        sent(hb1.at[pl.ds(0, 24)], hs.at[1])

    for g in range(2):
        send_x(g, bpx, brx, bxs, bxr)
    def across_done(sending, arriving):
        got(arriving, hdr)
        sent(sending, hds)

    pl.when(c == 0)(lambda: across_done(hb0, hb1))
    pl.when(c == 1)(lambda: across_done(hb1, hb0))

    raw = jnp.zeros((ROWS, TOKENS), f32)
    for part, block in enumerate((hb0, hb1, hb1, hb1)):
        at = part * SHARE
        skip = max(at - SHARE, 0)
        h2[...] = block[:, :, skip:skip + SHARE].astype(f32).reshape(TOKENS, SHARE).astype(bf16)
        raw += lax.dot_general(
            wv[:, at:at + SHARE], h2[...], (((1,), (1,)), ((), ())), preferred_element_type=f32)
    squash = jnp.tanh(raw * (1.0 / softcap))
    terms = jnp.exp(softcap * squash)

    slope = 1.0 - squash * squash
    den_b[dp] = jnp.concatenate([
        jnp.sum(terms, axis=0, keepdims=True),
        jnp.sum(jnp.where(onehot, terms, 0.0), axis=0, keepdims=True),
        jnp.sum(jnp.where(onehot, slope, 0.0), axis=0, keepdims=True)], axis=1)
    each(PLANE, lambda k: copy(
        den_b.at[dp], den_b.at[dp], dbs, dbr, lax.rem(dp + k, PLANE), vo).start())
    lt[0:ROWS, :] = jnp.where(onehot, 0.0, terms * slope).astype(bf16)
    for_sibling(lt, ds_, dr_, c_s, c_r)
    for g in range(2):
        own_half(g, lt, dr_, c_r, px, pz, rz, zs, zr, py, r1y, y1s, y1r)
        send_x(g, px, rx, xs, xr)
    got(den_b.at[pl.ds(0, PLANE - 1)], dbr)
    den_a[vo] = jnp.sum(den_b[...], axis=0)
    each(LINE, lambda k: copy(
        den_a.at[vo], den_a.at[vo], das, dar, dp, lax.rem(vo + k, LINE)).start())

    def summed(own, arriving, count, at, recv):
        total = own.astype(f32)
        got(arriving.at[pl.ds(0, count - 1)], recv)
        for k in range(1, count):
            total += arriving[at(k)].astype(f32)
        return total

    def x_sum(g, own, arriving, recv):
        total = own[g, x].astype(f32)
        got(arriving.at[g, pl.ds(0, 3)], recv.at[g])
        for k in (1, 2, 3):
            total += arriving[g, xp(k)].astype(f32)
        return total.astype(bf16)

    def over_x(rows, arriving, s_sem, r_sem):
        for k in (1, 2, 3):
            copy(rows.at[xp(k)], arriving.at[x], s_sem, r_sem, at_x(k), vo).start()

    def over_z(g, rows, arriving, s_sem, r_sem):
        def body(i, carry):
            @pl.when(i != z)
            def _():
                copy(rows.at[i], arriving.at[z], s_sem, r_sem, dp, i * NC + c).start()

            return carry

        lax.fori_loop(4 * g, 4 * g + 4, body, 0)

    def second_step(by_x, by_z, by_y, rx_, rz_, ry_, xr_, zr_, yr_, qx_, qz_, qy_, r2x_, r2z_, r2y_,
                    x2s_, x2r_, z2s_, z2r_, y2s_, y2r_):
        qy_[...] = summed(by_y[y], ry_, NY, yp, yr_).astype(bf16)
        over_x(qy_, r2y_, y2s_, y2r_)
        qz_[...] = summed(by_z[z], rz_, NZ, zp, zr_).astype(bf16)
        over_x(qz_, r2z_, z2s_, z2r_)
        for g in range(2):
            qx_[4 * g:4 * g + 4] = x_sum(g, by_x, rx_, xr_)
            over_z(g, qx_, r2x_, x2s_, x2r_)

    second_step(bpx, bpz, bpy, brx, brz, br1y, bxr, bzr, by1r, bqx, bqz, bqy, br2x, br2z, br2y,
                bx2s, bx2r, bz2s, bz2r, by2s, by2r)
    second_step(px, pz, py, rx, rz, r1y, xr, zr, y1r, qx, qz, qy, r2x, r2z, r2y, x2s, x2r, z2s, z2r, y2s, y2r)
    label[XU + ZU:] = summed(bqy[x], br2y, NX, xp, by2r).astype(bf16)
    label[LXU:XU + ZU] = summed(bqz[x], br2z, NX, xp, bz2r).astype(bf16)
    label[0:LXU] = summed(bqx[z], br2x, NZ, zp, bx2r).astype(bf16)

    got(den_a.at[pl.ds(0, LINE - 1)], dar)
    sums = jnp.sum(den_a[...], axis=0)
    inverse = 1.0 / sums[:, 0:TOKENS]
    at_label = ((sums[:, TOKENS:2 * TOKENS] * inverse - 1.0) * sums[:, 2 * TOKENS:]).astype(bf16).astype(f32)

    def joined(total, first, last):
        return (total * inverse + label[first:last].astype(f32) * at_label).astype(bf16)

    sy[...] = joined(summed(qy[x], r2y, NX, xp, y2r), XU + ZU, UNITS)

    @pl.when(z != y)
    def _():
        copy(sy, r3y.at[z], y3s, y3r, dp, y * NC + c).start()

    ry[y, XU:] = joined(summed(qz[x], r2z, NX, xp, z2r), XU, XU + ZU)
    ry[y, 0:XU] = joined(summed(qx[z], r2x, NZ, zp, x2r), 0, XU)

    each(NY, lambda k: copy(ry.at[y], ry.at[y], ys, yr, at_y(k), vo).start())

    @pl.when(z == y)
    def _():
        got(r3y.at[pl.ds(0, NZ - 1)], y3r)
        done = sy[...].astype(f32)
        for k in range(1, NZ):
            done += r3y[zp(k)].astype(f32)
        yb[...] = done.astype(bf16)
        each(NY, lambda k: copy(yb, yb, y4s, y4r, at_y(k), vo).start())

    got(ry.at[pl.ds(0, NY - 1)], yr)
    total = ry[0].astype(f32)
    for k in range(1, NY):
        total += ry[k].astype(f32)
    taker_dp, taker_core = y * NX + 2 * c + x // 2, lax.rem(x, 2)
    holds = z == y
    own_taker = (taker_dp == dp) & (taker_core == c)
    shift = lax.rem(z, 2) * 8 + c * 36

    def quarter(v):
        return gb.at[pl.ds(shift + v * UNITS, UNITS)]

    @pl.when(z != y)
    def _():
        got(yb, y4r)

    gb[pl.ds(shift + x * UNITS, XU + ZU)] = total.astype(bf16)
    gb[pl.ds(shift + x * UNITS + XU + ZU, YU)] = yb[...]

    @pl.when(holds)
    def _():
        def body(k, carry):
            @pl.when(jnp.logical_not(own_taker) | (k > 0))
            def _():
                copy(quarter(x), rb, bs, br, taker_dp, zp(k) * NC + taker_core).start()

            return carry

        lax.fori_loop(0, NZ, body, 0)

    for k in (1, 2, 3):
        copy(quarter(x), quarter(x), gs, gr.at[x], at_x(k), vo).start()
    copy(quarter(x), quarter(x), gds, gdr.at[x], dp, sib).start()

    @pl.when(holds & own_taker)
    def _():
        rb[...] = gb[pl.ds(shift + x * UNITS, UNITS)]

    for k in (1, 3, 2):
        got(quarter(xp(k)), gr.at[xp(k)])
        copy(quarter(xp(k)), quarter(xp(k)), gds, gdr.at[xp(k)], dp, sib).start()

    block = gb[pl.ds(shift, 36)].astype(f32).reshape(CHUNK, TOKENS).astype(bf16)
    token = lax.broadcasted_iota(jnp.int32, (8, TOKENS), 1)
    mine = jnp.where(token == dp * 8 + lax.broadcasted_iota(jnp.int32, (8, TOKENS), 0), 1.0, 0.0).astype(bf16)
    grads[...] = lax.dot_general(
        mine, block, (((1,), (1,)), ((), ())), preferred_element_type=f32).astype(bf16)
    gram_rows[...] = jnp.zeros_like(gram_rows)

    for v in range(NX):
        got(quarter(v), gdr.at[v])

    @pl.when(jnp.logical_not(holds & own_taker))
    def _():
        got(rb, br)

    rows = rb[...].astype(f32).reshape(72, TOKENS).astype(bf16)
    line_row = lax.broadcasted_iota(jnp.int32, (128, 72), 0)
    column = lax.broadcasted_iota(jnp.int32, (128, 72), 1)
    place, within = line_row // 16, lax.rem(line_row, 16)
    pick = jnp.where((within < 9) & (column == place * 9 + within), 1.0, 0.0).astype(bf16)
    spread_rows = jnp.dot(pick, rows, preferred_element_type=f32).astype(bf16)
    columns = gb[...].astype(f32).reshape(640, TOKENS).astype(bf16)
    gram = lax.dot_general(spread_rows, columns, (((1,), (1,)), ((), ())), preferred_element_type=f32)
    tb[...] = gram.reshape(NZ, 16, 640).astype(bf16)

    def to_place(k, carry):
        place = zp(k)

        @pl.when(NZ * c + place != vo)
        def _():
            copy(tb.at[place], rt.at[z], ts, tr.at[z], dp, NZ * c + place).start()

        return carry

    lax.fori_loop(0, NZ, to_place, 0)
    sender = z // 4

    @pl.when(sender == c)
    def _():
        rt[z] = tb[lax.rem(vo, NZ)]

    for v in range(NZ):
        @pl.when(v * NC + sender != vo)
        def _():
            got(rt.at[0], tr.at[v])

        at = v * NC * CHUNK // 128 * 128
        gram_rows[:, at:at + 640] += rt[v].astype(f32)[0:9]

    sent(tb.at[pl.ds(0, NZ - 1)], ts)

    @pl.when(sender != c)
    def _():
        sent(tb.at[0], ts)

    @pl.when(holds)
    def _():
        sent(gb.at[pl.ds(0, (NZ - 1) * UNITS)], bs)

    @pl.when(holds & jnp.logical_not(own_taker))
    def _():
        sent(rb, bs)

    sent(gb.at[pl.ds(0, NX * UNITS)], gds)
    sent(gb.at[pl.ds(0, 3 * UNITS)], gs)
    sent(ry.at[pl.ds(0, NY - 1)], ys)
    sent(den_b.at[pl.ds(0, PLANE - 1)], dbs)
    sent(den_a.at[pl.ds(0, LINE - 1)], das)

    @pl.when(z == y)
    def _():
        sent(r3y.at[pl.ds(0, NY - 1)], y4s)

    @pl.when(z != y)
    def _():
        sent(sy, y3s)

    for rows, sem in ((py, y1s), (bpy, by1s), (pz, zs), (bpz, bzs), (qx, x2s), (bqx, bx2s)):
        sent(rows.at[pl.ds(0, NZ - 1)], sem)
    for rows, sem in ((qz, z2s), (qy, y2s), (bqz, bz2s), (bqy, by2s)):
        sent(rows.at[pl.ds(0, NX - 1)], sem)
    for rows, sem in ((px, xs), (bpx, bxs)):
        sent(rows.at[:, pl.ds(0, NX - 1)], sem)
    sent(ds_, c_s)
    sent(bds, bc_s)


def update(gram_rows, grads_in, factor, new_factor, grads):
    scale = (1.0 - decay_rate) * (D / TOKENS)
    new_factor[...] = decay_rate * factor[...] + scale * gram_rows[...]
    grads[...] = grads_in[...]


def on_device(hidden, labels, head_weight, factor_rows):
    vmem = pl.BlockSpec(memory_space=pltpu.VMEM)
    dma = pltpu.SemaphoreType.DMA

    def buf(*shape, dtype=bf16):
        return pltpu.VMEM(shape, dtype)

    any_space = pl.BlockSpec(memory_space=pl.ANY)
    gram_rows, grads = pl.pallas_call(
        kernel,
        out_shape=(
            jax.ShapeDtypeStruct(factor_rows.shape, f32),
            jax.ShapeDtypeStruct((TOKENS // PLANE, CHUNK), bf16),
        ),
        in_specs=[any_space] * 3,
        out_specs=(vmem, vmem),
        scratch_shapes=[
            buf(TOKENS // PLANE, D), buf(1, TOKENS, dtype=jnp.int32), buf(ROWS, D), buf(D, PADDED), buf(PLANE, 8, SHARE), buf(PLANE, 8, D - SHARE), buf(TOKENS, SHARE), buf(PADDED, TOKENS),
            buf(NZ, NX, UNITS, 8, TOKENS), buf(NZ, NX, UNITS, 8, TOKENS),
            buf(2, NX, 4, XU, 8, TOKENS), buf(NZ, NX, ZU, 8, TOKENS),
            buf(2, NX, 4, XU, 8, TOKENS), buf(NZ, NX, ZU, 8, TOKENS),
            buf(NZ, XU, 8, TOKENS), buf(NX, ZU, 8, TOKENS),
            buf(NZ, XU, 8, TOKENS), buf(NX, ZU, 8, TOKENS),
            buf(NY, XU + ZU, 8, TOKENS), buf(80, 8, TOKENS), buf(UNITS, 8, TOKENS),
            buf(NZ, 16, 640), buf(NZ, 16, 640),
            buf(LINE, 1, 3 * TOKENS, dtype=f32), buf(PLANE, 1, 3 * TOKENS, dtype=f32), buf(PADDED, TOKENS),
            buf(NZ, NX, UNITS, 8, TOKENS), buf(NZ, NX, UNITS, 8, TOKENS),
            buf(2, NX, 4, LXU, 8, TOKENS), buf(NZ, NX, LZU, 8, TOKENS),
            buf(2, NX, 4, LXU, 8, TOKENS), buf(NZ, NX, LZU, 8, TOKENS),
            buf(NY, NX, YU, 8, TOKENS), buf(NY, NX, YU, 8, TOKENS), buf(NY, NX, YU, 8, TOKENS), buf(NY, NX, YU, 8, TOKENS),
            buf(NX, YU, 8, TOKENS), buf(NX, YU, 8, TOKENS), buf(YU, 8, TOKENS), buf(NZ, YU, 8, TOKENS),
            buf(YU, 8, TOKENS),
            buf(NZ, LXU, 8, TOKENS), buf(NX, LZU, 8, TOKENS), buf(NX, YU, 8, TOKENS),
            buf(NZ, LXU, 8, TOKENS), buf(NX, LZU, 8, TOKENS), buf(NX, YU, 8, TOKENS), buf(UNITS, 8, TOKENS),
            dma, dma((2,)), dma((2,)), dma((32,)), dma, dma, dma, dma, dma, dma, dma, dma((NZ,)),
            dma, dma((2,)), dma, dma, dma, dma, dma, dma, dma, dma, dma, dma((NX,)),
            dma, dma, dma, dma((NZ,)), dma, dma((NX,)), dma, dma((NZ,)), dma, dma((2,)), dma, dma,
            dma, dma, dma, dma, dma, dma, dma, dma, dma, dma, dma, dma,
            dma, dma, dma, dma,
        ],
        compiler_params=pltpu.CompilerParams(
            collective_id=0, has_side_effects=True, vmem_limit_bytes=56 * 2**20),
        cost_estimate=pl.CostEstimate(flops=4 * 500 * 256 * 4608, bytes_accessed=6 * 2**20, transcendentals=2 * 500 * 256),
    )(hidden, labels.reshape(1, TOKENS), head_weight)
    return pl.pallas_call(
        update,
        out_shape=(
            jax.ShapeDtypeStruct(factor_rows.shape, f32),
            jax.ShapeDtypeStruct(grads.shape, bf16),
        ),
        in_specs=[vmem] * 3,
        out_specs=(vmem, vmem),
    )(gram_rows, grads, factor_rows)


def solution(mesh):
    placed = (P("dp", None), P(), P(("dp", "vocab"), None), P(("dp", "vocab"), None))
    return jax.shard_map(
        on_device,
        mesh=mesh,
        in_specs=placed,
        out_specs=(P(("dp", "vocab"), None), P("dp", "vocab")),
        check_vma=False,
    )
```

```python
import jax
import jax.numpy as jnp
from jax import lax
from jax.experimental import pallas as pl
from jax.experimental.pallas import tpu as pltpu
from jax.sharding import PartitionSpec as P

softcap = 30.0
decay_rate = 0.95

NX, NY, NZ, NC = 4, 8, 8, 2
PLANE, LINE = NX * NY, NZ * NC
D, TOKENS, ROWS = 4608, 256, 500
PADDED = 512
SHARE = D // 4
CHUNK = D // LINE
UNITS = CHUNK // 8 // NX
XU, ZU, YU = 5, 2, 2
LXU, LZU = 2, 5
MESH = pl.DeviceIdType.MESH
f32, bf16 = jnp.float32, jnp.bfloat16


def kernel(
    hidden_in, labels_in, head, gram_rows, grads,
    hidden, labels, wv, wt, hb0, hb1, h2, lt, ds_, dr_, px, pz, rx, rz, qx, qz, r2x, r2z, ry, gb, rb, tb, rt, den_a, den_b, lab, bds, bdr, bpx, bpz, brx, brz,
    py, r1y, bpy, br1y, qy, r2y, sy, r3y, yb,
    bqx, bqz, bqy, br2x, br2z, br2y, label, logits,
    w_sem, in_sem, hs, hr, hds, hdr, das, dar, dbs, dbr, c_s, c_r, xs, xr, zs, zr, x2s, x2r, z2s, z2r,
    ys, yr, gs, gr, bs, br, ts, tr, gds, gdr, bc_s, bc_r, bxs, bxr, bzs, bzr,
    y1s, y1r, by1s, by1r, y2s, y2r, y3s, y3r, y4s, y4r, bx2s, bx2r, bz2s, bz2r, by2s, by2r,
):
    dp, vo = lax.axis_index("dp"), lax.axis_index("vocab")
    x, y = lax.rem(dp, NX), dp // NX
    c, z = lax.rem(vo, NC), vo // NC
    sib = vo + 1 - 2 * c

    def copy(src, dst, send, recv, to_dp, to_vo):
        return pltpu.make_async_remote_copy(
            src_ref=src, dst_ref=dst, send_sem=send, recv_sem=recv, device_id=(to_dp, to_vo), device_id_type=MESH
        )

    def got(ref, recv):
        copy(ref, ref, recv, recv, dp, sib).wait_recv()

    def sent(ref, send):
        copy(ref, ref, send, send, dp, sib).wait_send()

    def each(count, body):
        lax.fori_loop(1, count, lambda k, carry: (body(k), carry)[1], 0)

    def xp(k):
        return lax.rem(x + k, NX)

    def yp(k):
        return lax.rem(y + k + NY, NY)

    def zp(k):
        return lax.rem(z + k, NZ)

    def at_x(k):
        return y * NX + xp(k)

    def at_y(k):
        return yp(k) * NX + x

    def at_z(k):
        return zp(k) * NC + c

    w_copy = pltpu.make_async_copy(head, wv, w_sem)
    hidden_copy = pltpu.make_async_copy(hidden_in, hidden, in_sem.at[0])
    labels_copy = pltpu.make_async_copy(labels_in, labels, in_sem.at[1])
    hidden_copy.start()
    labels_copy.start()
    w_copy.start()
    gb[...] = jnp.zeros_like(gb)

    barrier = pltpu.get_barrier_semaphore()
    each(LINE, lambda k: pl.semaphore_signal(
        barrier, inc=1, device_id=(dp, lax.rem(vo + k, LINE)), device_id_type=MESH))
    each(PLANE, lambda k: pl.semaphore_signal(
        barrier, inc=1, device_id=(lax.rem(dp + k, PLANE), vo), device_id_type=MESH))
    wt[:, PADDED - 128:] = jnp.zeros((D, 128), bf16)
    lt[PADDED - 16:, :] = jnp.zeros((16, TOKENS), bf16)
    lab[PADDED - 16:, :] = jnp.zeros((16, TOKENS), bf16)
    pl.semaphore_wait(barrier, LINE + PLANE - 2)
    hidden_copy.wait()
    labels_copy.wait()

    def transpose_head(first, last):
        def body(b, carry):
            at = pl.multiple_of(b * 256, 256)
            wt[pl.ds(at, 256), 0:ROWS] = wv[:, pl.ds(at, 256)].T
            return carry

        lax.fori_loop(first, last, body, 0)

    def partial_of(rows, i, core):
        start = pl.multiple_of((i * NC + core) * CHUNK, 32)
        product = jnp.dot(wt[pl.ds(start, CHUNK), :], rows[...], preferred_element_type=f32)
        return product.reshape(NX, UNITS, 8, TOKENS)

    def for_sibling(rows, out, arriving, s_sem, r_sem):
        def body(i, carry):
            out[i] = partial_of(rows, i, 1 - c).astype(bf16)
            copy(out.at[i], arriving.at[i], s_sem, r_sem.at[i], dp, sib).start()
            return carry

        lax.fori_loop(0, NZ, body, 0)

    def own_half(g, rows, arriving, r_sem, by_x, by_z, z_arriving, zs_sem, zr_sem, by_y, y_arriving, ys_sem, yr_sem):
        def body(i, carry):
            total = partial_of(rows, i, c)
            got(arriving.at[i], r_sem.at[i])
            total = (total + arriving[i].astype(f32)).astype(bf16)
            for v in range(NX):
                by_x[g, v, i - 4 * g] = total[v, 0:by_x.shape[3]]
                by_z[i, v] = total[v, by_x.shape[3]:XU + ZU]
                by_y[i, v] = total[v, XU + ZU:]

            @pl.when(i != z)
            def _():
                copy(by_z.at[i], z_arriving.at[z], zs_sem, zr_sem, dp, i * NC + c).start()

            @pl.when(i != y)
            def _():
                copy(by_y.at[i], y_arriving.at[y], ys_sem, yr_sem, i * NX + x, vo).start()

            return carry

        lax.fori_loop(4 * g, 4 * g + 4, body, 0)

    def send_x(g, by_x, arriving, s_sem, r_sem):
        for k in (1, 2, 3):
            copy(by_x.at[g, xp(k)], arriving.at[g, x], s_sem, r_sem.at[g], at_x(k), vo).start()

    onehot = lax.broadcasted_iota(jnp.int32, (ROWS, TOKENS), 0) == labels[...] - (dp * LINE + vo) * ROWS

    def label_first():
        lab[0:ROWS, :] = onehot.astype(f32).astype(bf16)
        for_sibling(lab, bds, bdr, bc_s, bc_r)

    def label_second():
        for g in range(2):
            own_half(g, lab, bdr, bc_r, bpx, bpz, brz, bzs, bzr, bpy, br1y, by1s, by1r)

    @pl.when(c == 0)
    def _():
        hb0[dp] = hidden[:, 0:SHARE]
        for k in (1, 2, 3):
            copy(hb0.at[dp], hb0.at[dp], hs.at[0], hr.at[dp], at_x(k), vo).start()
        w_copy.wait()
        transpose_head(0, 18)
        for k in (1, 2, 3):
            got(hb0.at[at_x(k)], hr.at[at_x(k)])

        def row(k):
            return hb0.at[pl.ds(yp(k) * NX, NX)]

        def row_copy(from_k, to_k):
            return copy(row(from_k), row(from_k), hs.at[1], hr.at[yp(from_k) * NX], at_y(to_k), vo)

        def across(k):
            copy(row(k), row(k), hds, hdr, dp, sib).start()

        def row_got(k):
            got(row(k), hr.at[yp(k) * NX])

        row_copy(0, 1).start()
        row_copy(0, -1).start()
        row_copy(0, 4).start()
        across(0)
        label_first()
        row_got(-1)
        row_copy(-1, 1).start()
        row_got(1)
        row_copy(1, -1).start()
        across(-1)
        across(1)
        label_second()
        row_got(4)
        row_copy(4, 1).start()
        row_copy(4, -1).start()
        across(4)
        for k in (2, -2, 3, -3):
            row_got(k)
            across(k)
        sent(hb0.at[pl.ds(0, 3)], hs.at[0])
        sent(hb0.at[pl.ds(0, 28)], hs.at[1])

    @pl.when(c == 1)
    def _():
        hb1[dp] = hidden[:, SHARE:]

        def own(k):
            return hb1.at[at_y(k)]

        def spread(k):
            for i in (1, 2, 3):
                copy(own(k), own(k), hs.at[1], hr.at[at_y(k)], yp(0) * NX + xp(i), vo).start()

        for k in (1, -1, 2, -2, 3, -3, 4):
            copy(own(0), own(0), hs.at[0], hr.at[dp], at_y(k), vo).start()
        spread(0)
        w_copy.wait()
        transpose_head(0, 18)
        for k in (1, -1):
            got(own(k), hr.at[at_y(k)])
            spread(k)
        label_first()
        for k in (2, -2, 3, -3, 4):
            got(own(k), hr.at[at_y(k)])
            spread(k)
        label_second()

        for k in (0, 1, -1, 2, -2, 3, -3, 4):
            for i in (1, 2, 3):
                slot = yp(k) * NX + xp(i)
                got(hb1.at[slot], hr.at[slot])
            rows = hb1.at[pl.ds(yp(k) * NX, NX)]
            copy(rows, rows, hds, hdr, dp, sib).start()
        sent(hb1.at[pl.ds(0, 7)], hs.at[0])
        sent(hb1.at[pl.ds(0, 24)], hs.at[1])

    for g in range(2):
        send_x(g, bpx, brx, bxs, bxr)

    def logits_of(block, first):
        total = None
        for part in range(block.shape[2] // SHARE):
            at = first + part * SHARE
            h2[...] = block[:, :, part * SHARE:(part + 1) * SHARE].astype(f32).reshape(TOKENS, SHARE).astype(bf16)
            product = lax.dot_general(
                wv[:, at:at + SHARE], h2[...], (((1,), (1,)), ((), ())), preferred_element_type=f32)
            total = product if total is None else total + product
        return total

    @pl.when(c == 0)
    def _():
        logits[...] = logits_of(hb0, 0)
        got(hb1, hdr)
        logits[...] += logits_of(hb1, SHARE)

    @pl.when(c == 1)
    def _():
        logits[...] = logits_of(hb1, SHARE)
        got(hb0, hdr)
        logits[...] += logits_of(hb0, 0)

    raw = logits[...]
    squash = jnp.tanh(raw * (1.0 / softcap))
    terms = jnp.exp(softcap * squash)

    slope = 1.0 - squash * squash
    den_b[dp] = jnp.concatenate([
        jnp.sum(terms, axis=0, keepdims=True),
        jnp.sum(jnp.where(onehot, terms, 0.0), axis=0, keepdims=True),
        jnp.sum(jnp.where(onehot, slope, 0.0), axis=0, keepdims=True)], axis=1)
    each(PLANE, lambda k: copy(
        den_b.at[dp], den_b.at[dp], dbs, dbr, lax.rem(dp + k, PLANE), vo).start())
    lt[0:ROWS, :] = jnp.where(onehot, 0.0, terms * slope).astype(bf16)
    for_sibling(lt, ds_, dr_, c_s, c_r)
    for g in range(2):
        own_half(g, lt, dr_, c_r, px, pz, rz, zs, zr, py, r1y, y1s, y1r)
        send_x(g, px, rx, xs, xr)
    got(den_b.at[pl.ds(0, PLANE - 1)], dbr)
    den_a[vo] = jnp.sum(den_b[...], axis=0)
    each(LINE, lambda k: copy(
        den_a.at[vo], den_a.at[vo], das, dar, dp, lax.rem(vo + k, LINE)).start())

    def summed(own, arriving, count, at, recv):
        total = own.astype(f32)
        got(arriving.at[pl.ds(0, count - 1)], recv)
        for k in range(1, count):
            total += arriving[at(k)].astype(f32)
        return total

    def x_sum(g, own, arriving, recv):
        total = own[g, x].astype(f32)
        got(arriving.at[g, pl.ds(0, 3)], recv.at[g])
        for k in (1, 2, 3):
            total += arriving[g, xp(k)].astype(f32)
        return total.astype(bf16)

    def over_x(rows, arriving, s_sem, r_sem):
        for k in (1, 2, 3):
            copy(rows.at[xp(k)], arriving.at[x], s_sem, r_sem, at_x(k), vo).start()

    def over_z(g, rows, arriving, s_sem, r_sem):
        def body(i, carry):
            @pl.when(i != z)
            def _():
                copy(rows.at[i], arriving.at[z], s_sem, r_sem, dp, i * NC + c).start()

            return carry

        lax.fori_loop(4 * g, 4 * g + 4, body, 0)

    def second_step(by_x, by_z, by_y, rx_, rz_, ry_, xr_, zr_, yr_, qx_, qz_, qy_, r2x_, r2z_, r2y_,
                    x2s_, x2r_, z2s_, z2r_, y2s_, y2r_):
        qy_[...] = summed(by_y[y], ry_, NY, yp, yr_).astype(bf16)
        over_x(qy_, r2y_, y2s_, y2r_)
        qz_[...] = summed(by_z[z], rz_, NZ, zp, zr_).astype(bf16)
        over_x(qz_, r2z_, z2s_, z2r_)
        for g in range(2):
            qx_[4 * g:4 * g + 4] = x_sum(g, by_x, rx_, xr_)
            over_z(g, qx_, r2x_, x2s_, x2r_)

    second_step(bpx, bpz, bpy, brx, brz, br1y, bxr, bzr, by1r, bqx, bqz, bqy, br2x, br2z, br2y,
                bx2s, bx2r, bz2s, bz2r, by2s, by2r)
    second_step(px, pz, py, rx, rz, r1y, xr, zr, y1r, qx, qz, qy, r2x, r2z, r2y, x2s, x2r, z2s, z2r, y2s, y2r)
    label[XU + ZU:] = summed(bqy[x], br2y, NX, xp, by2r).astype(bf16)
    label[LXU:XU + ZU] = summed(bqz[x], br2z, NX, xp, bz2r).astype(bf16)
    label[0:LXU] = summed(bqx[z], br2x, NZ, zp, bx2r).astype(bf16)

    got(den_a.at[pl.ds(0, LINE - 1)], dar)
    sums = jnp.sum(den_a[...], axis=0)
    inverse = 1.0 / sums[:, 0:TOKENS]
    at_label = ((sums[:, TOKENS:2 * TOKENS] * inverse - 1.0) * sums[:, 2 * TOKENS:]).astype(bf16).astype(f32)

    def joined(total, first, last):
        return (total * inverse + label[first:last].astype(f32) * at_label).astype(bf16)

    sy[...] = joined(summed(qy[x], r2y, NX, xp, y2r), XU + ZU, UNITS)

    @pl.when(z != y)
    def _():
        copy(sy, r3y.at[z], y3s, y3r, dp, y * NC + c).start()

    ry[y, XU:] = joined(summed(qz[x], r2z, NX, xp, z2r), XU, XU + ZU)
    ry[y, 0:XU] = joined(summed(qx[z], r2x, NZ, zp, x2r), 0, XU)

    each(NY, lambda k: copy(ry.at[y], ry.at[y], ys, yr, at_y(k), vo).start())

    @pl.when(z == y)
    def _():
        got(r3y.at[pl.ds(0, NZ - 1)], y3r)
        done = sy[...].astype(f32)
        for k in range(1, NZ):
            done += r3y[zp(k)].astype(f32)
        yb[...] = done.astype(bf16)
        each(NY, lambda k: copy(yb, yb, y4s, y4r, at_y(k), vo).start())

    got(ry.at[pl.ds(0, NY - 1)], yr)
    total = ry[0].astype(f32)
    for k in range(1, NY):
        total += ry[k].astype(f32)
    taker_dp, taker_core = y * NX + 2 * c + x // 2, lax.rem(x, 2)
    holds = z == y
    own_taker = (taker_dp == dp) & (taker_core == c)
    shift = lax.rem(z, 2) * 8 + c * 36

    def quarter(v):
        return gb.at[pl.ds(shift + v * UNITS, UNITS)]

    @pl.when(z != y)
    def _():
        got(yb, y4r)

    gb[pl.ds(shift + x * UNITS, XU + ZU)] = total.astype(bf16)
    gb[pl.ds(shift + x * UNITS + XU + ZU, YU)] = yb[...]

    @pl.when(holds)
    def _():
        def body(k, carry):
            @pl.when(jnp.logical_not(own_taker) | (k > 0))
            def _():
                copy(quarter(x), rb, bs, br, taker_dp, zp(k) * NC + taker_core).start()

            return carry

        lax.fori_loop(0, NZ, body, 0)

    for k in (1, 2, 3):
        copy(quarter(x), quarter(x), gs, gr.at[x], at_x(k), vo).start()
    copy(quarter(x), quarter(x), gds, gdr.at[x], dp, sib).start()

    @pl.when(holds & own_taker)
    def _():
        rb[...] = gb[pl.ds(shift + x * UNITS, UNITS)]

    for k in (1, 3, 2):
        got(quarter(xp(k)), gr.at[xp(k)])
        copy(quarter(xp(k)), quarter(xp(k)), gds, gdr.at[xp(k)], dp, sib).start()

    block = gb[pl.ds(shift, 36)].astype(f32).reshape(CHUNK, TOKENS).astype(bf16)
    token = lax.broadcasted_iota(jnp.int32, (8, TOKENS), 1)
    mine = jnp.where(token == dp * 8 + lax.broadcasted_iota(jnp.int32, (8, TOKENS), 0), 1.0, 0.0).astype(bf16)
    grads[...] = lax.dot_general(
        mine, block, (((1,), (1,)), ((), ())), preferred_element_type=f32).astype(bf16)
    gram_rows[...] = jnp.zeros_like(gram_rows)

    for v in range(NX):
        got(quarter(v), gdr.at[v])

    @pl.when(jnp.logical_not(holds & own_taker))
    def _():
        got(rb, br)

    rows = rb[...].astype(f32).reshape(72, TOKENS).astype(bf16)
    line_row = lax.broadcasted_iota(jnp.int32, (128, 72), 0)
    column = lax.broadcasted_iota(jnp.int32, (128, 72), 1)
    place, within = line_row // 16, lax.rem(line_row, 16)
    pick = jnp.where((within < 9) & (column == place * 9 + within), 1.0, 0.0).astype(bf16)
    spread_rows = jnp.dot(pick, rows, preferred_element_type=f32).astype(bf16)
    columns = gb[...].astype(f32).reshape(640, TOKENS).astype(bf16)
    gram = lax.dot_general(spread_rows, columns, (((1,), (1,)), ((), ())), preferred_element_type=f32)
    tb[...] = gram.reshape(NZ, 16, 640).astype(bf16)

    def to_place(k, carry):
        place = zp(k)

        @pl.when(NZ * c + place != vo)
        def _():
            copy(tb.at[place], rt.at[z], ts, tr.at[z], dp, NZ * c + place).start()

        return carry

    lax.fori_loop(0, NZ, to_place, 0)
    sender = z // 4

    @pl.when(sender == c)
    def _():
        rt[z] = tb[lax.rem(vo, NZ)]

    for v in range(NZ):
        @pl.when(v * NC + sender != vo)
        def _():
            got(rt.at[0], tr.at[v])

        at = v * NC * CHUNK // 128 * 128
        gram_rows[:, at:at + 640] += rt[v].astype(f32)[0:9]

    @pl.when(c == 0)
    def _():
        sent(hb0, hds)

    @pl.when(c == 1)
    def _():
        sent(hb1, hds)

    sent(tb.at[pl.ds(0, NZ - 1)], ts)

    @pl.when(sender != c)
    def _():
        sent(tb.at[0], ts)

    @pl.when(holds)
    def _():
        sent(gb.at[pl.ds(0, (NZ - 1) * UNITS)], bs)

    @pl.when(holds & jnp.logical_not(own_taker))
    def _():
        sent(rb, bs)

    sent(gb.at[pl.ds(0, NX * UNITS)], gds)
    sent(gb.at[pl.ds(0, 3 * UNITS)], gs)
    sent(ry.at[pl.ds(0, NY - 1)], ys)
    sent(den_b.at[pl.ds(0, PLANE - 1)], dbs)
    sent(den_a.at[pl.ds(0, LINE - 1)], das)

    @pl.when(z == y)
    def _():
        sent(r3y.at[pl.ds(0, NY - 1)], y4s)

    @pl.when(z != y)
    def _():
        sent(sy, y3s)

    for rows, sem in ((py, y1s), (bpy, by1s), (pz, zs), (bpz, bzs), (qx, x2s), (bqx, bx2s)):
        sent(rows.at[pl.ds(0, NZ - 1)], sem)
    for rows, sem in ((qz, z2s), (qy, y2s), (bqz, bz2s), (bqy, by2s)):
        sent(rows.at[pl.ds(0, NX - 1)], sem)
    for rows, sem in ((px, xs), (bpx, bxs)):
        sent(rows.at[:, pl.ds(0, NX - 1)], sem)
    sent(ds_, c_s)
    sent(bds, bc_s)


def update(gram_rows, grads_in, factor, new_factor, grads):
    scale = (1.0 - decay_rate) * (D / TOKENS)
    new_factor[...] = decay_rate * factor[...] + scale * gram_rows[...]
    grads[...] = grads_in[...]


def on_device(hidden, labels, head_weight, factor_rows):
    vmem = pl.BlockSpec(memory_space=pltpu.VMEM)
    dma = pltpu.SemaphoreType.DMA

    def buf(*shape, dtype=bf16):
        return pltpu.VMEM(shape, dtype)

    any_space = pl.BlockSpec(memory_space=pl.ANY)
    gram_rows, grads = pl.pallas_call(
        kernel,
        out_shape=(
            jax.ShapeDtypeStruct(factor_rows.shape, f32),
            jax.ShapeDtypeStruct((TOKENS // PLANE, CHUNK), bf16),
        ),
        in_specs=[any_space] * 3,
        out_specs=(vmem, vmem),
        scratch_shapes=[
            buf(TOKENS // PLANE, D), buf(1, TOKENS, dtype=jnp.int32), buf(ROWS, D), buf(D, PADDED), buf(PLANE, 8, SHARE), buf(PLANE, 8, D - SHARE), buf(TOKENS, SHARE), buf(PADDED, TOKENS),
            buf(NZ, NX, UNITS, 8, TOKENS), buf(NZ, NX, UNITS, 8, TOKENS),
            buf(2, NX, 4, XU, 8, TOKENS), buf(NZ, NX, ZU, 8, TOKENS),
            buf(2, NX, 4, XU, 8, TOKENS), buf(NZ, NX, ZU, 8, TOKENS),
            buf(NZ, XU, 8, TOKENS), buf(NX, ZU, 8, TOKENS),
            buf(NZ, XU, 8, TOKENS), buf(NX, ZU, 8, TOKENS),
            buf(NY, XU + ZU, 8, TOKENS), buf(80, 8, TOKENS), buf(UNITS, 8, TOKENS),
            buf(NZ, 16, 640), buf(NZ, 16, 640),
            buf(LINE, 1, 3 * TOKENS, dtype=f32), buf(PLANE, 1, 3 * TOKENS, dtype=f32), buf(PADDED, TOKENS),
            buf(NZ, NX, UNITS, 8, TOKENS), buf(NZ, NX, UNITS, 8, TOKENS),
            buf(2, NX, 4, LXU, 8, TOKENS), buf(NZ, NX, LZU, 8, TOKENS),
            buf(2, NX, 4, LXU, 8, TOKENS), buf(NZ, NX, LZU, 8, TOKENS),
            buf(NY, NX, YU, 8, TOKENS), buf(NY, NX, YU, 8, TOKENS), buf(NY, NX, YU, 8, TOKENS), buf(NY, NX, YU, 8, TOKENS),
            buf(NX, YU, 8, TOKENS), buf(NX, YU, 8, TOKENS), buf(YU, 8, TOKENS), buf(NZ, YU, 8, TOKENS),
            buf(YU, 8, TOKENS),
            buf(NZ, LXU, 8, TOKENS), buf(NX, LZU, 8, TOKENS), buf(NX, YU, 8, TOKENS),
            buf(NZ, LXU, 8, TOKENS), buf(NX, LZU, 8, TOKENS), buf(NX, YU, 8, TOKENS), buf(UNITS, 8, TOKENS), buf(ROWS, TOKENS, dtype=f32),
            dma, dma((2,)), dma((2,)), dma((32,)), dma, dma, dma, dma, dma, dma, dma, dma((NZ,)),
            dma, dma((2,)), dma, dma, dma, dma, dma, dma, dma, dma, dma, dma((NX,)),
            dma, dma, dma, dma((NZ,)), dma, dma((NX,)), dma, dma((NZ,)), dma, dma((2,)), dma, dma,
            dma, dma, dma, dma, dma, dma, dma, dma, dma, dma, dma, dma,
            dma, dma, dma, dma,
        ],
        compiler_params=pltpu.CompilerParams(
            collective_id=0, has_side_effects=True, vmem_limit_bytes=56 * 2**20),
        cost_estimate=pl.CostEstimate(flops=4 * 500 * 256 * 4608, bytes_accessed=6 * 2**20, transcendentals=2 * 500 * 256),
    )(hidden, labels.reshape(1, TOKENS), head_weight)
    return pl.pallas_call(
        update,
        out_shape=(
            jax.ShapeDtypeStruct(factor_rows.shape, f32),
            jax.ShapeDtypeStruct(grads.shape, bf16),
        ),
        in_specs=[vmem] * 3,
        out_specs=(vmem, vmem),
    )(gram_rows, grads, factor_rows)


def solution(mesh):
    placed = (P("dp", None), P(), P(("dp", "vocab"), None), P(("dp", "vocab"), None))
    return jax.shard_map(
        on_device,
        mesh=mesh,
        in_specs=placed,
        out_specs=(P(("dp", "vocab"), None), P("dp", "vocab")),
        check_vma=False,
    )
```
